256 devices in a mesh: seq: 16 (over z_hi, x), ch: 16 (over z_lo, y, core).
Axes of the slice: x: 4, y: 4, z: 8 (z_hi: 4, z_lo: 2; z = z_hi * 2 + z_lo), core: 2. Of those that a mesh axis runs over, the one named last changes fastest.
Arguments:
- strands: bfloat16 [2, 32768, 512], P(None, ('seq', 'ch')), may hold values from -24 to 24
- cotangent: bfloat16 [2, 32768, 512], P(None, ('seq', 'ch')), may hold values from -6 to 6
- proj_in: bfloat16 [512, 3072], P('ch'), may hold values from -0.25 to 0.25
- proj_out: bfloat16 [1024, 512], P('ch'), may hold values from -0.1875 to 0.1875
- short_taps: float32 [3072, 4], replicated, may hold values from -3 to 3
- filters: bfloat16 [64, 128], replicated, may hold values from -0.5 to 0.5
Outputs:
- strands_out: bfloat16 [2, 32768, 512], P(None, ('seq', 'ch'))
- grad_strands: bfloat16 [2, 32768, 512], P(None, ('seq', 'ch'))
- grad_proj_in: float32 [512, 3072], P('ch')
- grad_proj_out: float32 [1024, 512], P('ch')
- grad_short: float32 [3072, 4], P('ch')
- grad_filters: float32 [64, 128], P('ch')
The draws below stay inside these ranges and needn't reach their ends.
All inputs are finite; a program needn't handle non-finite values.
Results may differ from the reference program's by a relative error of at most 0.017.
Values may be sent and summed in bfloat16 or wider, within the bound.
A program may use at most 128 MiB of HBM per device.

```python
import jax
import jax.numpy as jnp
from jax import lax

STRAND = 512
INNER = 1024
SHORT = 4
TAPS = 128
GROUP = 16
GROUPS = 64
LENGTH = 32768


def raised(entries, rng, source, target, parts, factor):
    owner, partner = [(jnp.arange(entries.shape[dim]) // (entries.shape[dim] // parts)).reshape([-1 if axis == dim else 1 for axis in range(entries.ndim)]) for dim in (source, target)]
    chosen = jax.random.permutation(rng, parts)[partner]
    strong = (owner == chosen) | (owner == (partner + parts // 2) % parts)
    return jnp.where(strong, factor * entries, entries)


def block_levels(own_key, extent, cuts, low, high):
    def one(dim, blocks):
        steps = jax.random.uniform(jax.random.fold_in(jax.random.fold_in(own_key, 6), dim), (blocks,), jnp.float32, low / len(cuts), high / len(cuts))
        return jnp.repeat(jnp.exp(steps), extent[dim] // blocks).reshape((-1,) + (1,) * (len(extent) - dim - 1))

    level = one(*cuts[0])
    for cut in cuts[1:]:
        level = level * one(*cut)
    return level


def normal_values(rng, extent, deviation, most, cuts=(), kind=jnp.bfloat16):
    values = deviation * jax.random.normal(rng, extent, jnp.float32)
    if cuts:
        values = values * block_levels(rng, extent, cuts, -0.22, 0.18)
    return jnp.clip(values, -most, most).astype(kind)


def bell_draw_with(rng, dims, width, reach, split, heavy, kind=jnp.bfloat16):
    values = width * jax.random.normal(rng, dims, jnp.float32)
    if split:
        values = values * block_levels(rng, dims, split, -0.22, 0.18)
    return jnp.clip(raised(values, jax.random.fold_in(rng, 3), *heavy), -reach, reach).astype(kind)


def setup_inputs(seed: int = 0) -> dict:
    streams_of = jax.random.split(jax.random.key(seed), 7)
    return {
        "strands": bell_draw_with(streams_of[0], (2, LENGTH, STRAND), 1.0, 24.0, ((1, 256),), (1, 2, 256, 6.0)),
        "cotangent": normal_values(streams_of[1], (2, LENGTH, STRAND), 1.0, 6.0, ((1, 256),)),
        "proj_in": normal_values(streams_of[2], (STRAND, 3 * INNER), STRAND ** -0.5, 0.25, ((0, 16),)),
        "proj_out": normal_values(streams_of[3], (INNER, STRAND), INNER ** -0.5, 0.1875, ((0, 16),)),
        "short_taps": normal_values(streams_of[4], (3 * INNER, SHORT), 0.5, 3.0, (), jnp.float32),
        "filters": normal_values(streams_of[5], (GROUPS, TAPS), TAPS ** -0.5, 0.5),
    }


exact_precision = lax.Precision.HIGHEST

def reverse_both(segment):
    return segment[::-1, ::-1]

def toeplitz_table(filters):
    group_count = filters.shape[0]
    filter_tap_count = filters.shape[1]
    head_zero = jnp.zeros((group_count, 1), filters.dtype)
    tail_zero = jnp.zeros((group_count, 2 * filter_tap_count - 1), filters.dtype)
    pattern = jnp.concatenate([head_zero, filters[:, ::-1], tail_zero], axis=1)
    repeated = jnp.tile(pattern, (1, filter_tap_count))
    skewed = repeated[:, :filter_tap_count * (3 * filter_tap_count - 1)].reshape(group_count, filter_tap_count, 3 * filter_tap_count - 1)
    return skewed[:, :, :2 * filter_tap_count]

def windows_of(extended, filter_tap_count, group_size):
    ext_rows = extended.shape[0]
    channels = extended.shape[1]
    pieces = extended.reshape(ext_rows // filter_tap_count, filter_tap_count, channels // group_size, group_size)
    return jnp.concatenate([pieces[:-1], pieces[1:]], axis=1)

def long_conv(extended, toeplitz, group_size):
    windows = windows_of(extended, toeplitz.shape[1], group_size)
    output = jnp.einsum('gij,bjgc->bigc', toeplitz.astype(jnp.float32), windows.astype(jnp.float32), precision=exact_precision)
    return output.reshape(-1, extended.shape[1])

def unskew(products):
    group_count = products.shape[0]
    filter_tap_count = products.shape[1]
    padded = jnp.pad(products, ((0, 0), (0, 0), (0, filter_tap_count - 1)))
    flattened = padded.reshape(group_count, filter_tap_count * (3 * filter_tap_count - 1))
    flattened = jnp.pad(flattened, ((0, 0), (0, filter_tap_count)))
    sheared = flattened.reshape(group_count, filter_tap_count, 3 * filter_tap_count)
    summed = lax.optimization_barrier(jnp.sum(sheared, axis=1))
    return summed[:, 1:filter_tap_count + 1][:, ::-1]

def filter_grad(extended, grad_conv, group_size, filter_tap_count):
    windows = windows_of(extended, filter_tap_count, group_size)
    grad_pieces = grad_conv.reshape(windows.shape[0], filter_tap_count, windows.shape[2], group_size)
    products = jnp.einsum('bigc,bjgc->gij', grad_pieces.astype(jnp.float32), windows.astype(jnp.float32), precision=exact_precision)
    return unskew(products)

def strand_pass(input_batch, cotangent, proj_in, proj_out, short_taps, toeplitz):
    row_count = input_batch.shape[0]
    short_len = short_taps.shape[1]
    projected = jnp.dot(input_batch, proj_in, preferred_element_type=jnp.float32).astype(jnp.bfloat16)
    proj_ext = jnp.concatenate([jnp.zeros((short_len - 1, projected.shape[1]), jnp.bfloat16), projected], axis=0)
    mixer_output = jnp.zeros((row_count, projected.shape[1]), jnp.float32)
    for shift_at in range(short_len):
        start_row = short_len - 1 - shift_at
        mixer_output = mixer_output + short_taps[:, shift_at] * proj_ext[start_row:start_row + row_count].astype(jnp.float32)
    query_part = mixer_output[:, :INNER]
    key_part = mixer_output[:, INNER:2 * INNER]
    value_part = mixer_output[:, 2 * INNER:]
    gated_prod = (key_part * value_part).astype(jnp.bfloat16)
    gated_ext = jnp.concatenate([jnp.zeros((TAPS, INNER), jnp.bfloat16), gated_prod], axis=0)
    conv_out = long_conv(gated_ext, toeplitz, GROUP)
    hidden = (query_part * conv_out).astype(jnp.bfloat16)
    result = jnp.dot(hidden, proj_out, preferred_element_type=jnp.float32).astype(jnp.bfloat16)
    grad_hidden = jnp.dot(cotangent, proj_out.T, preferred_element_type=jnp.float32).astype(jnp.bfloat16)
    part_out = jnp.dot(hidden.T, cotangent, preferred_element_type=jnp.float32)
    hidden_grad = grad_hidden.astype(jnp.float32)
    query_gradient = hidden_grad * conv_out
    grad_conv = (hidden_grad * query_part).astype(jnp.bfloat16)
    grad_ext = jnp.concatenate([jnp.zeros((TAPS, INNER), jnp.bfloat16), grad_conv[::-1]], axis=0)
    grad_gated = long_conv(grad_ext, toeplitz, GROUP)[::-1]
    part_filters = filter_grad(gated_ext, grad_conv, GROUP, TAPS)
    grad_mixed = jnp.concatenate([query_gradient, grad_gated * value_part, grad_gated * key_part], axis=1).astype(jnp.bfloat16)
    mixed_ext = jnp.concatenate([grad_mixed, jnp.zeros((short_len - 1, grad_mixed.shape[1]), jnp.bfloat16)], axis=0)
    grad_sum = jnp.zeros((row_count, grad_mixed.shape[1]), jnp.float32)
    for shift_at in range(short_len):
        grad_sum = grad_sum + short_taps[:, shift_at] * mixed_ext[shift_at:shift_at + row_count].astype(jnp.float32)
    projection_gradient = grad_sum.astype(jnp.bfloat16)
    mixed_grad = grad_mixed.astype(jnp.float32)
    columns = []
    for shift_at in range(short_len):
        start_row = short_len - 1 - shift_at
        columns.append(lax.optimization_barrier(jnp.sum(proj_ext[start_row:start_row + row_count].astype(jnp.float32) * mixed_grad, axis=0)))
    part_short = jnp.stack(columns, axis=1)
    grad_inputs = jnp.dot(projection_gradient, proj_in.T, preferred_element_type=jnp.float32).astype(jnp.bfloat16)
    partial_input = jnp.dot(input_batch.T, projection_gradient, preferred_element_type=jnp.float32)
    return (result, grad_inputs, partial_input, part_out, part_short, part_filters)

def reference(strands, cotangent, proj_in, proj_out, short_taps, filters):
    toeplitz = toeplitz_table(filters)
    strand_zero = strand_pass(strands[0], cotangent[0], proj_in, proj_out, short_taps, toeplitz)
    strand_one = strand_pass(reverse_both(strands[1]), reverse_both(cotangent[1]), proj_in, proj_out, short_taps, toeplitz)
    grad_scale = float(LENGTH) ** (-0.5)
    strands_out = jnp.stack([strand_zero[0], reverse_both(strand_one[0])])
    grad_strands = jnp.stack([strand_zero[1], reverse_both(strand_one[1])])
    grad_proj_in = (strand_zero[2] + strand_one[2]) * grad_scale
    grad_proj_out = (strand_zero[3] + strand_one[3]) * grad_scale
    grad_short = (strand_zero[4] + strand_one[4]) * grad_scale
    grad_filters = (strand_zero[5] + strand_one[5]) * grad_scale
    return (strands_out, grad_strands, grad_proj_in, grad_proj_out, grad_short, grad_filters)
```

```python
import functools

import jax
import jax.numpy as jnp
from jax import lax
from jax.experimental import pallas as pl
from jax.experimental.pallas import tpu as pltpu
from jax.sharding import PartitionSpec as P

F32 = jnp.float32
BF16 = jnp.bfloat16
NN = (((1,), (0,)), ((), ()))
NT = (((1,), (1,)), ((), ()))
TN = (((0,), (0,)), ((), ()))


def mm(a, b, dims=NN):
    return lax.dot_general(a, b, dims, preferred_element_type=F32)


def lane_group(shape):
    return (lax.broadcasted_iota(jnp.int32, shape, 1) % 128) // 16


def build_tables(filters, TF, TB):
    t = lax.broadcasted_iota(jnp.int32, (128, 256), 0)
    k = lax.broadcasted_iota(jnp.int32, (128, 256), 1)
    to_f = jnp.where(t + k == 128, 1.0, 0.0).astype(BF16)
    to_b = jnp.where(t == k, 1.0, 0.0).astype(BF16)
    pat_f = mm(filters, to_f)
    pat_b = mm(filters, to_b)
    for g in range(32):
        for pat, table in ((pat_f, TF), (pat_b, TB)):
            rows = jnp.broadcast_to(pat[g:g + 1], (128, 256))
            skewed = pltpu.roll(rows, 0, 1, stride=1, stride_axis=0)
            table[g // 8, pl.ds((g % 8) * 128, 128), :] = skewed.astype(BF16)


def anti_identity(n):
    r = lax.broadcasted_iota(jnp.int32, (n, n), 0)
    c = lax.broadcasted_iota(jnp.int32, (n, n), 1)
    return jnp.where(r + c == n - 1, 1.0, 0.0).astype(BF16)


def diag(products, rows):
    group = lane_group((rows, products.shape[1]))
    out = products[0:rows]
    for g in range(1, 8):
        out = jnp.where(group == g, products[g * rows:(g + 1) * rows], out)
    return out


def shifted(x, j):
    if j == 0:
        return x
    return pltpu.roll(x, j % x.shape[0], 0)


def compute_chunk(k, U, C, Win, Wout, taps_ref, TF, TB, UT, HID, GP, PIN, PSH, PFIL):
    w = Win[k]
    wo = Wout[pl.ds(pl.multiple_of(128 * k, 128), 128), :]
    taps = taps_ref[k]
    tf = TF[k]
    tb = TB[k]
    proj, gated, gc, keys, values, queries, ghs = [], [], [], [], [], [], []
    for s in range(2):
        sign = 1 if s == 0 else -1
        kv_at = 0 if s == 0 else 128
        q_at = 128 - kv_at
        pkv = mm(U[s, pl.ds(kv_at, 416), :], w[:, 128:]).astype(BF16)
        pq = mm(U[s, pl.ds(q_at, 416), :], w[:, :128]).astype(BF16)
        gh = mm(C[s], wo, NT).astype(BF16).astype(F32)
        pkv32 = pkv.astype(F32)
        pq32 = pq.astype(F32)
        mkv = jnp.zeros((416, 256), F32)
        mq = jnp.zeros((416, 128), F32)
        for j in range(4):
            mkv = mkv + taps[j:j + 1, 128:] * shifted(pkv32, sign * j)
            mq = mq + taps[j:j + 1, :128] * shifted(pq32, sign * j)
        key, value = mkv[:, :128], mkv[:, 128:]
        gated.append((key * value).astype(BF16))
        keys.append(key)
        values.append(value)
        queries.append(mq)
        ghs.append(gh)
        at = 16 if s == 0 else 0
        gc.append((gh * mq[at:at + 400]).astype(BF16))
        own_kv = 144 if s == 0 else 16
        own_q = 160 - own_kv
        proj.append((pq32[own_q:own_q + 256], pkv32[own_kv:own_kv + 256]))
    wf = jnp.concatenate([gated[0][:400], gc[1]], axis=1)
    f_parts, b_parts = [], []
    prods = None
    for blk in range(2):
        xf = wf[16 + 128 * blk:272 + 128 * blk]
        f_parts.append(diag(mm(tf, xf), 128))
        xb = jnp.concatenate([gc[0][128 * blk:128 * blk + 256], gated[1][16 + 128 * blk:272 + 128 * blk]], axis=1)
        b_parts.append(diag(mm(tb, xb), 128))
        left = jnp.concatenate([gc[0][128 * blk:128 * blk + 128], gated[1][16 + 128 * blk:144 + 128 * blk]], axis=1)
        left = mm(anti_identity(128), left).astype(BF16)
        group = lane_group((128, 256))
        masked = jnp.concatenate([jnp.where(group == g, left, jnp.zeros_like(left)) for g in range(8)], axis=0)
        term = mm(masked, xf, NT)
        prods = term if prods is None else prods + term
    tf3 = tf.reshape(8, 128, 256)
    tb3 = tb.reshape(8, 128, 256)
    f_last = tf3[:, 112:].reshape(128, 256)
    f_first = tf3[:, :16].reshape(128, 256)
    b_last = tb3[:, 112:].reshape(128, 256)
    b_first = tb3[:, :16].reshape(128, 256)
    conv0_x = diag(mm(f_last, gated[0][160:416]), 16)
    gg1_x = diag(mm(f_first, gc[1][0:256]), 16)
    gg0_x = diag(mm(b_last, gc[0][144:400]), 16)
    conv1_x = diag(mm(b_first, gated[1][0:256]), 16)
    conv = [
        jnp.concatenate([f_parts[0][:, :128], f_parts[1][:, :128], conv0_x], axis=0),
        jnp.concatenate([conv1_x, b_parts[0][:, 128:], b_parts[1][:, 128:]], axis=0),
    ]
    gg = [
        jnp.concatenate([b_parts[0][:, :128], b_parts[1][:, :128], gg0_x], axis=0),
        jnp.concatenate([gg1_x, f_parts[0][:, 128:], f_parts[1][:, 128:]], axis=0),
    ]
    short = [jnp.zeros((1, 384), F32) for _ in range(4)]
    for s in range(2):
        sign = 1 if s == 0 else -1
        own = 0 if s == 0 else 16
        q_at = 16 if s == 0 else 128
        kv_at = 144 if s == 0 else 0
        gh_at = 0 if s == 0 else 128
        query = queries[s][q_at:q_at + 272]
        hidden = (query[own:own + 256] * conv[s][own:own + 256]).astype(BF16)
        HID[k, pl.ds(256 * s, 256), :] = hidden
        gm = jnp.concatenate(
            [
                ghs[s][gh_at:gh_at + 272] * conv[s],
                gg[s] * values[s][kv_at:kv_at + 272],
                gg[s] * keys[s][kv_at:kv_at + 272],
            ],
            axis=1,
        ).astype(BF16).astype(F32)
        p_own = jnp.concatenate(proj[s], axis=1)
        total = jnp.zeros((256, 384), F32)
        for j in range(4):
            moved = shifted(gm, -sign * j)[own:own + 256]
            total = total + taps[j:j + 1] * moved
            short[j] = short[j] + jnp.sum(p_own * moved, axis=0, keepdims=True)
        GP[k, pl.ds(256 * s, 256), :] = total.astype(BF16)
    PSH[k] = jnp.concatenate(short, axis=0)
    PIN[k] = mm(UT[...], GP[k])
    rows = []
    for g in range(8):
        r = pltpu.roll(prods[128 * g:128 * g + 128], 129, 1, stride=1, stride_axis=0)
        rows.append(jnp.sum(r, axis=0, keepdims=True))
    PFIL[k] = jnp.concatenate(rows, axis=0)


MESH = pl.DeviceIdType.MESH


def remote(src, dst, send, recv, device):
    copy = pltpu.make_async_remote_copy(
        src_ref=src, dst_ref=dst, send_sem=send, recv_sem=recv, device_id=device, device_id_type=MESH
    )
    copy.start()
    return copy


def wait_bytes(ref, sem):
    pltpu.make_async_copy(ref, ref, sem).wait()


def at_coords(x, y, z, c):
    return ((z // 2) * 4 + x, (z % 2) * 8 + y * 2 + c)


def at_chip(p, c):
    return (p // 8, (p % 8) * 2 + c)


def halves(tile, other):
    lane = lax.broadcasted_iota(jnp.int32, tile.shape, 1)
    low = jnp.where(lane < 64, tile, pltpu.roll(other, 64, 1))
    high = jnp.where(lane < 64, pltpu.roll(tile, 64, 1), other)
    return low, high


def kernel(
    scale,
    strands, cotangent, proj_in, proj_out, taps_ref, filters_ref,
    out_ref, grad_ref, gin_ref, gout_ref, gshort_ref, gfil_ref,
    U, C, W, WO, WSEND, TF, TB, UT, HID, GP, PIN, PSH, PFIL, PART, OUTP, RP,
    SZ, RZ, SXY, RXY, S2, ZH, FIN, FSEND,
    SZ4, RZ4, SXY4, RXY4, S24, ZH4, FIN4, FSEND4, SMALL,
    pair_send, pair_recv, halo_send, halo_recv, fwd_send, fwd_recv,
    w_send, w_recv, wp_send, wp_recv,
    z_send, z_recv, xy_send, xy_recv, zh_send, zh_recv, xg_send, xg_recv, sm_send, sm_recv, op_send, op_recv,
):
    seq, ch = lax.axis_index("seq"), lax.axis_index("ch")
    z_hi, x = seq // 4, seq % 4
    z_lo, y, c = ch // 8, (ch // 2) % 4, ch % 2
    z = z_hi * 2 + z_lo
    b = z_lo * 4 + y
    chip = seq * 8 + b
    before, after = (chip + 127) % 128, (chip + 1) % 128
    partner = at_coords(x, y, z, 1 - c)
    y_up, y_down = at_coords(x, (y + 1) % 4, z, c), at_coords(x, (y + 3) % 4, z, c)
    z_up, z_down = at_coords(x, y, (z + 1) % 8, c), at_coords(x, y, (z + 7) % 8, c)

    barrier = pltpu.get_barrier_semaphore()
    peers = [partner, z_up, z_down]
    for dx in range(4):
        for dy in range(4):
            if dx or dy:
                peers.append(at_coords((x + dx) % 4, (y + dy) % 4, z, c))
    for d in range(1, 4):
        peers.append(at_coords(x, y, (z + 2 * d) % 8, c))
        peers.append(at_coords((x + d) % 4, y, z, 1 - c))
    for q in (before, after):
        peers.append(at_chip(q, 0))
        peers.append(at_chip(q, 1))
    for peer in peers:
        pl.semaphore_signal(barrier, inc=1, device_id=peer, device_id_type=MESH)

    flip = anti_identity(512)
    own = pl.multiple_of(144 + 128 * c, 16)
    own_c0 = pl.multiple_of(128 * c, 16)
    U[0, pl.ds(own, 128), :] = strands[0]
    U[1, pl.ds(own, 128), :] = mm(strands[1], flip).astype(BF16)
    C[0, pl.ds(own_c0, 128), :] = cotangent[0]
    C[1, pl.ds(own, 128), :] = mm(cotangent[1], flip).astype(BF16)
    my_rows = pl.multiple_of(64 * b + 32 * c, 32)
    for k in range(4):
        for s in range(3):
            left = proj_in[:, pl.ds(s * 1024 + k * 256, 128)].astype(F32)
            right = proj_in[:, pl.ds(s * 1024 + k * 256 + 128, 128)].astype(F32)
            even, odd = halves(left, right)
            first = c == 0
            W[k, pl.ds(my_rows, 32), pl.ds(128 * s, 128)] = jnp.where(first, even, odd).astype(BF16)
            WSEND[k, :, pl.ds(128 * s, 128)] = jnp.where(first, odd, even).astype(BF16)
    WO[pl.ds(pl.multiple_of(64 * b, 64), 64), :] = proj_out[...]
    pl.semaphore_wait(barrier, len(peers))

    wp = [
        remote(WSEND.at[k], W.at[k, pl.ds(my_rows, 32), :], wp_send.at[k], wp_recv.at[k], partner) for k in range(4)
    ]
    far = jnp.where(c == 0, before, after)
    near = jnp.where(c == 0, after, before)
    big_at = pl.multiple_of(jnp.where(c == 0, 400, 16), 16)
    small_src = pl.multiple_of(own + jnp.where(c == 0, 112, 0), 16)
    small_at = pl.multiple_of(jnp.where(c == 0, 0, 528), 16)
    halo = []
    for s in range(2):
        halo.append(remote(
            U.at[s, pl.ds(own, 128), :], U.at[s, pl.ds(big_at, 128), :],
            halo_send.at[s], halo_recv.at[1 - c], at_chip(far, s)))
        halo.append(remote(
            U.at[s, pl.ds(small_src, 16), :], U.at[s, pl.ds(small_at, 16), :],
            halo_send.at[2 + s], halo_recv.at[2 + c], at_chip(near, s)))
    c_own = pl.multiple_of(jnp.where(c == 0, 0, 272), 16)
    c_big = pl.multiple_of(jnp.where(c == 0, 256, 16), 16)
    halo.append(remote(
        C.at[c, pl.ds(c_own, 128), :], C.at[c, pl.ds(c_big, 128), :],
        halo_send.at[4], halo_recv.at[4], at_chip(far, c)))
    c_small_src = pl.multiple_of(jnp.where(c == 0, 144 + 112, 128), 16)
    c_small = pl.multiple_of(jnp.where(c == 0, 0, 384), 16)
    halo.append(remote(
        C.at[1 - c, pl.ds(c_small_src, 16), :], C.at[1 - c, pl.ds(c_small, 16), :],
        halo_send.at[5], halo_recv.at[5], at_chip(near, 1 - c)))
    pair = [
        remote(U.at[s, pl.ds(own, 128), :], U.at[s, pl.ds(own, 128), :], pair_send.at[s], pair_recv.at[s], partner)
        for s in range(2)
    ]
    pair.append(remote(
        C.at[0, pl.ds(own_c0, 128), :], C.at[0, pl.ds(own_c0, 128), :], pair_send.at[2], pair_recv.at[2], partner))
    pair.append(remote(
        C.at[1, pl.ds(own, 128), :], C.at[1, pl.ds(own, 128), :], pair_send.at[3], pair_recv.at[3], partner))

    def shard(m, yy, zz, half=None):
        at, size = 64 * (zz * 4 + yy), 64
        if half is not None:
            at, size = at + 32 * half, 32
        rows = pl.ds(pl.multiple_of(at, 32), size)
        return WO.at[rows, :] if m == 4 else W.at[m, rows, :]

    y_next, y_prev, y_far = (y + 1) % 4, (y + 3) % 4, (y + 2) % 4
    order = (0, 4, 1, 2, 3)

    def gather_first(m):
        mine = shard(m, y, z_lo)
        remote(mine, mine, w_send.at[m], w_recv.at[m, 0], y_up)
        remote(mine, mine, w_send.at[m], w_recv.at[m, 1], y_down)
        low, high = shard(m, y, z_lo, 0), shard(m, y, z_lo, 1)
        remote(low, low, w_send.at[m], w_recv.at[m, 4], z_up)
        remote(high, high, w_send.at[m], w_recv.at[m, 4], z_down)

    def gather_second(m):
        wait_bytes(shard(m, y_prev, z_lo), w_recv.at[m, 0])
        wait_bytes(shard(m, y_next, z_lo), w_recv.at[m, 1])
        low, high = shard(m, y_prev, z_lo, 0), shard(m, y_prev, z_lo, 1)
        remote(low, low, w_send.at[m], w_recv.at[m, 2], y_up)
        remote(low, low, w_send.at[m], w_recv.at[m, 4], z_up)
        remote(high, high, w_send.at[m], w_recv.at[m, 4], z_down)
        low, high = shard(m, y_next, z_lo, 0), shard(m, y_next, z_lo, 1)
        remote(high, high, w_send.at[m], w_recv.at[m, 3], y_down)
        remote(low, low, w_send.at[m], w_recv.at[m, 4], z_up)
        remote(high, high, w_send.at[m], w_recv.at[m, 4], z_down)

    def gather_third(m):
        low, high = shard(m, y_far, z_lo, 0), shard(m, y_far, z_lo, 1)
        wait_bytes(low, w_recv.at[m, 2])
        remote(low, low, w_send.at[m], w_recv.at[m, 4], z_up)
        wait_bytes(high, w_recv.at[m, 3])
        remote(high, high, w_send.at[m], w_recv.at[m, 4], z_down)

    def gather_last(m):
        rows = WO if m == 4 else W.at[m]
        wait_bytes(rows.at[pl.ds(0, 256), :], w_recv.at[m, 4])

    def gather_sent(m):
        rows = WO if m == 4 else W.at[m]
        wait_bytes(rows.at[pl.ds(0, 448), :], w_send.at[m])

    for m in order:
        if m < 4:
            wp[m].wait()
        gather_first(m)

    build_tables(filters_ref[...], TF, TB)

    for m in order:
        gather_second(m)
    wait_bytes(U.at[c, pl.ds(16, 128), :], halo_recv.at[0])
    wait_bytes(U.at[c, pl.ds(400, 128), :], halo_recv.at[1])
    wait_bytes(U.at[c, pl.ds(0, 16), :], halo_recv.at[2])
    wait_bytes(U.at[c, pl.ds(528, 16), :], halo_recv.at[3])
    wait_bytes(C.at[c, pl.ds(c_big, 128), :], halo_recv.at[4])
    wait_bytes(C.at[c, pl.ds(pl.multiple_of(jnp.where(c == 0, 384, 0), 16), 16), :], halo_recv.at[5])
    c_halo = pl.multiple_of(jnp.where(c == 0, 256, 0), 16)
    c_halo_other = pl.multiple_of(jnp.where(c == 0, 0, 256), 16)
    fwd = []
    for i, at in enumerate((0, 400)):
        rows = U.at[c, pl.ds(at, 144), :]
        fwd.append(remote(rows, rows, fwd_send.at[i], fwd_recv.at[i], partner))
    rows = C.at[c, pl.ds(c_halo, 144), :]
    fwd.append(remote(rows, rows, fwd_send.at[2], fwd_recv.at[2], partner))
    for m in order:
        gather_third(m)
    for copy in pair:
        copy.wait()
    for copy in halo:
        copy.wait_send()
    for i, at in enumerate((0, 400)):
        wait_bytes(U.at[1 - c, pl.ds(at, 144), :], fwd_recv.at[i])
    wait_bytes(C.at[1 - c, pl.ds(c_halo_other, 144), :], fwd_recv.at[2])
    for copy in fwd:
        copy.wait_send()

    @pl.when(chip == 0)
    def _():
        U[:, pl.ds(0, 144), :] = jnp.zeros((2, 144, 512), BF16)
        C[1, pl.ds(0, 144), :] = jnp.zeros((144, 512), BF16)

    @pl.when(chip == 127)
    def _():
        U[:, pl.ds(400, 144), :] = jnp.zeros((2, 144, 512), BF16)
        C[0, pl.ds(256, 144), :] = jnp.zeros((144, 512), BF16)

    for s in range(2):
        UT[:, pl.ds(256 * s, 256)] = jnp.transpose(U[s, pl.ds(144, 256), :])
    for m in order:
        gather_last(m)
        gather_sent(m)

    def stages(part, sz, rz, sxy, rxy, s2, zh, fsend, width, base):
        def z_start(k):
            rows = pl.ds(pl.multiple_of((1 - z_lo) * 256, 256), 256)
            sz[k] = part(k, rows).astype(BF16).reshape(4, 2, 32, width)
            remote(sz.at[k, :, 0], rz.at[k, :, 0], z_send.at[base + k], z_recv.at[base + k, 0], z_up)
            remote(sz.at[k, :, 1], rz.at[k, :, 1], z_send.at[base + k], z_recv.at[base + k, 1], z_down)

        def xy_start(k):
            wait_bytes(rz.at[k, :, 0], z_recv.at[base + k, 0])
            wait_bytes(rz.at[k, :, 1], z_recv.at[base + k, 1])
            wait_bytes(sz.at[k], z_send.at[base + k])
            rows = pl.ds(pl.multiple_of(z_lo * 256, 256), 256)
            total = part(k, rows) + rz[k].astype(F32).reshape(256, width)
            sxy[k] = total.astype(BF16).reshape(4, 4, 16, width)
            for dx in range(4):
                for dy in range(4):
                    if dx or dy:
                        xx, yy = (x + dx) % 4, (y + dy) % 4
                        remote(sxy.at[k, yy, xx], rxy.at[k, 4 * dx + dy - 1],
                               xy_send.at[base + k], xy_recv.at[base + k], at_coords(xx, yy, z, c))

        def zh_start(k):
            wait_bytes(rxy.at[k], xy_recv.at[base + k])
            wait_bytes(rxy.at[k], xy_send.at[base + k])
            total = sxy[k, y, x].astype(F32)
            for i in range(15):
                total = total + rxy[k, i].astype(F32)
            zh[k, z_hi] = total.astype(BF16)
            for d in range(1, 4):
                remote(zh.at[k, z_hi], zh.at[k, z_hi], zh_send.at[base + k], zh_recv.at[base + k],
                       at_coords(x, y, (z + 2 * d) % 8, c))

        def zh_end(k):
            wait_bytes(zh.at[k, pl.ds(0, 3)], zh_recv.at[base + k])
            wait_bytes(zh.at[k, pl.ds(0, 3)], zh_send.at[base + k])
            total = zh[k, 0].astype(F32)
            for i in range(1, 4):
                total = total + zh[k, i].astype(F32)
            fsend[k] = total * scale

        return z_start, xy_start, zh_start, zh_end

    in_z, in_xy, in_zh, in_end = stages(
        lambda k, rows: PIN[k, rows, :], SZ, RZ, SXY, RXY, S2, ZH, FSEND, 384, 0)
    out_z, out_xy, out_zh, out_end = stages(
        lambda k, rows: PART[rows, :], SZ4, RZ4, SXY4, RXY4, S24, ZH4, FSEND4, 640, 4)

    target = x // 2
    row_at = pl.multiple_of(16 * (x % 2), 16)

    def in_gather(k):
        in_end(k)
        place = FIN.at[k, c, pl.ds(row_at, 16), :]
        for d in range(1, 4):
            remote(FSEND.at[k], place, xg_send.at[k], xg_recv.at[k], at_coords((x + d) % 4, y, z, target))

        @pl.when(c == target)
        def _():
            pltpu.make_async_copy(FSEND.at[k], place, xg_recv.at[k]).start()

        @pl.when(c != target)
        def _():
            remote(FSEND.at[k], place, xg_send.at[k], xg_recv.at[k], partner)

    def in_last(k):
        wait_bytes(FIN.at[k], xg_recv.at[k])
        wait_bytes(FSEND.at[pl.ds(0, 3)], xg_send.at[k])

        @pl.when(c != target)
        def _():
            wait_bytes(FSEND.at[k], xg_send.at[k])

        for s in range(3):
            low, high = halves(FIN[k, 0, :, pl.ds(128 * s, 128)], FIN[k, 1, :, pl.ds(128 * s, 128)])
            gin_ref[:, pl.ds(s * 1024 + k * 256, 128)] = low
            gin_ref[:, pl.ds(s * 1024 + k * 256 + 128, 128)] = high

    def out_gather():
        out_end(0)
        place = FIN4.at[x]
        for d in range(1, 4):
            remote(FSEND4.at[0], place, xg_send.at[4], xg_recv.at[4], at_coords((x + d) % 4, y, z, c))

        @pl.when(x == 0)
        def _():
            small = FSEND4.at[0, :, pl.ds(512, 128)]
            for d in range(1, 4):
                remote(small, SMALL, sm_send, sm_recv, at_coords((x + d) % 4, y, z, 1 - c))
            remote(small, SMALL, sm_send, sm_recv, partner)

        FIN4[x] = FSEND4[0]

    def out_last():
        wait_bytes(FIN4.at[pl.ds(0, 3)], xg_recv.at[4])
        wait_bytes(FIN4.at[pl.ds(0, 3)], xg_send.at[4])
        wait_bytes(SMALL, sm_recv)

        @pl.when(x == 0)
        def _():
            wait_bytes(FIN4.at[0, :, pl.ds(0, 512)], sm_send)

        gout_ref[...] = FIN4[...].reshape(64, 640)[:, :512]
        mine = FIN4[0, :, pl.ds(512, 128)]
        theirs = SMALL[...]
        reversal = anti_identity(128).astype(F32)
        gfil_ref[...] = lax.dot_general(
            mine, reversal, NN, precision=lax.Precision.HIGHEST, preferred_element_type=F32)[8:12]
        even = jnp.where(c == 0, mine, theirs)
        odd = jnp.where(c == 0, theirs, mine)
        lane = lax.broadcasted_iota(jnp.int32, (4, 128), 1)

        def blocks(v):
            a, t = v[0:4], v[4:8]
            shifted_a, shifted_t = pltpu.roll(a, 64, 1), pltpu.roll(t, 64, 1)
            first = jnp.where(b % 2 == 0, a, shifted_a)
            second = jnp.where(b % 2 == 0, shifted_a, t)
            third = jnp.where(b % 2 == 0, t, shifted_t)
            return first, second, third

        e, o = blocks(even), blocks(odd)
        one = jnp.where(c == 0, e[0], o[1])
        two = jnp.where(c == 0, o[0], e[2])
        three = jnp.where(c == 0, e[1], o[2])
        left = jnp.where(lane < 64, one, pltpu.roll(two, 64, 1))
        pad = jnp.zeros((124, 128), F32)
        gshort_ref[pl.ds(0, 128), :] = jnp.transpose(jnp.concatenate([left, pad], axis=0))[:, :4]
        gshort_ref[pl.ds(128, 64), :] = jnp.transpose(jnp.concatenate([three, pad], axis=0))[:64, :4]

    def body(k, carry):
        compute_chunk(k, U, C, W, WO, taps_ref, TF, TB, UT, HID, GP, PIN, PSH, PFIL)
        in_z(k)

        @pl.when(k >= 1)
        def _():
            in_xy(k - 1)

        @pl.when(k >= 2)
        def _():
            in_zh(k - 2)

        @pl.when(k >= 3)
        def _():
            in_gather(k - 3)

        return carry

    lax.fori_loop(0, 4, body, 0)

    for k in range(4):
        rows = pl.ds(128 * k, 128)
        part = mm(HID[k, pl.ds(0, 256), :], C[0, pl.ds(0, 256), :], TN)
        PART[rows, pl.ds(0, 512)] = part + mm(HID[k, pl.ds(256, 256), :], C[1, pl.ds(144, 256), :], TN)
    PART[:, pl.ds(512, 128)] = jnp.zeros((512, 128), F32)
    for i in range(8):
        m = i // 2
        tiles = (3 * m, 3 * m + 1) if i % 2 == 0 else (3 * m + 1, 3 * m + 2)
        pieces = [PSH[t % 4, :, pl.ds(128 * (t // 4), 128)] for t in tiles]
        taps_first = pltpu.roll(PFIL[m], 255, 1)[4 * (i % 2):4 * (i % 2) + 4, :128]
        PART[pl.ds(64 * i, 16), pl.ds(512, 128)] = jnp.concatenate(
            pieces + [taps_first, jnp.zeros((4, 128), F32)], axis=0)
    out_z(0)
    in_xy(3)
    in_zh(2)
    in_gather(1)
    res = mm(HID[0], WO[pl.ds(0, 128), :])
    for k in range(1, 4):
        res = res + mm(HID[k], WO[pl.ds(128 * k, 128), :])
    OUTP[0] = res
    out_xy(0)
    in_zh(3)
    in_gather(2)
    res = mm(GP[0], W[0], NT)
    for k in range(1, 4):
        res = res + mm(GP[k], W[k], NT)
    OUTP[1] = res
    other_rows = 128 * (1 - c)
    op = []
    for o in range(2):
        for s in range(2):
            rows = pl.ds(pl.multiple_of(256 * s + other_rows, 128), 128)
            op.append(remote(OUTP.at[o, rows, :], RP.at[o, s], op_send.at[o, s], op_recv.at[o, s], partner))
    out_zh(0)
    in_gather(3)
    out_gather()
    for copy in op:
        copy.wait()
    for o, ref in enumerate((out_ref, grad_ref)):
        for s in range(2):
            rows = pl.ds(pl.multiple_of(256 * s + 128 * c, 128), 128)
            value = (OUTP[o, rows, :] + RP[o, s]).astype(BF16)
            ref[s] = value if s == 0 else mm(value, flip).astype(BF16)
    for k in range(4):
        in_last(k)
    out_last()


def shards(strands, cotangent, proj_in, proj_out, short_taps, filters):
    c = lax.axis_index("ch") % 2
    taps = lax.dynamic_index_in_dim(short_taps.reshape(3, 8, 2, 64, 4), c, 2, keepdims=False)
    taps = taps.reshape(3, 4, 128, 4).transpose(1, 3, 0, 2).reshape(4, 4, 384)
    fil = lax.dynamic_index_in_dim(filters.reshape(8, 2, 4, 128), c, 1, keepdims=False).reshape(32, 128)
    length = strands.shape[1] * lax.axis_size(("seq", "ch"))
    scale = float(length) ** (-0.5)
    vmem = pl.BlockSpec(memory_space=pltpu.VMEM)
    dma = pltpu.SemaphoreType.DMA
    outs = (
        jax.ShapeDtypeStruct((2, 128, 512), BF16),
        jax.ShapeDtypeStruct((2, 128, 512), BF16),
        jax.ShapeDtypeStruct((32, 3072), F32),
        jax.ShapeDtypeStruct((64, 512), F32),
        jax.ShapeDtypeStruct((192, 4), F32),
        jax.ShapeDtypeStruct((4, 128), F32),
    )
    scratch = [
        pltpu.VMEM((2, 544, 512), BF16),
        pltpu.VMEM((2, 400, 512), BF16),
        pltpu.VMEM((4, 512, 384), BF16),
        pltpu.VMEM((512, 512), BF16),
        pltpu.VMEM((4, 32, 384), BF16),
        pltpu.VMEM((4, 1024, 256), BF16),
        pltpu.VMEM((4, 1024, 256), BF16),
        pltpu.VMEM((512, 512), BF16),
        pltpu.VMEM((4, 512, 128), BF16),
        pltpu.VMEM((4, 512, 384), BF16),
        pltpu.VMEM((4, 512, 384), F32),
        pltpu.VMEM((4, 4, 384), F32),
        pltpu.VMEM((4, 8, 256), F32),
        pltpu.VMEM((512, 640), F32),
        pltpu.VMEM((2, 512, 512), F32),
        pltpu.VMEM((2, 2, 128, 512), F32),
    ]
    for n, width in ((4, 384), (1, 640)):
        scratch += [
            pltpu.VMEM((n, 4, 2, 32, width), BF16),
            pltpu.VMEM((n, 4, 2, 32, width), BF16),
            pltpu.VMEM((n, 4, 4, 16, width), BF16),
            pltpu.VMEM((n, 15, 16, width), BF16),
            pltpu.VMEM((8, 128), F32),
            pltpu.VMEM((n, 4, 16, width), BF16),
            pltpu.VMEM((4, 2, 32, 384) if n == 4 else (4, 16, 640), F32),
            pltpu.VMEM((n, 16, width), F32),
        ]
    scratch.append(pltpu.VMEM((16, 128), F32))
    scratch += [
        dma((4,)), dma((4,)), dma((6,)), dma((6,)), dma((3,)), dma((3,)),
        dma((5,)), dma((5, 5)), dma((4,)), dma((4,)),
        dma((5,)), dma((5, 2)), dma((5,)), dma((5,)), dma((5,)), dma((5,)), dma((5,)), dma((5,)),
        dma, dma, dma((2, 2)), dma((2, 2)),
    ]
    return pl.pallas_call(
        functools.partial(kernel, scale),
        out_shape=outs,
        in_specs=[vmem] * 6,
        out_specs=tuple([vmem] * 6),
        scratch_shapes=scratch,
        compiler_params=pltpu.CompilerParams(
            collective_id=0, has_side_effects=True, vmem_limit_bytes=58 * 2**20
        ),
        cost_estimate=pl.CostEstimate(flops=9 * 10**9, bytes_accessed=4 * 10**6, transcendentals=0),
    )(strands, cotangent, proj_in, proj_out, taps, fil)


def solution(mesh):
    placed = P(None, ("seq", "ch"), None)
    rows = P("ch", None)
    return jax.shard_map(
        shards,
        mesh=mesh,
        in_specs=(placed, placed, rows, rows, P(), P()),
        out_specs=(placed, placed, rows, rows, rows, rows),
        check_vma=False,
    )
```

```python
import functools

import jax
import jax.numpy as jnp
from jax import lax
from jax.experimental import pallas as pl
from jax.experimental.pallas import tpu as pltpu
from jax.sharding import PartitionSpec as P

F32 = jnp.float32
BF16 = jnp.bfloat16
NN = (((1,), (0,)), ((), ()))
NT = (((1,), (1,)), ((), ()))
TN = (((0,), (0,)), ((), ()))


def mm(a, b, dims=NN):
    return lax.dot_general(a, b, dims, preferred_element_type=F32)


def lane_group(shape):
    return (lax.broadcasted_iota(jnp.int32, shape, 1) % 128) // 16


def build_tables(filters, TF, TB):
    t = lax.broadcasted_iota(jnp.int32, (128, 256), 0)
    k = lax.broadcasted_iota(jnp.int32, (128, 256), 1)
    to_f = jnp.where(t + k == 128, 1.0, 0.0).astype(BF16)
    to_b = jnp.where(t == k, 1.0, 0.0).astype(BF16)
    pat_f = mm(filters, to_f)
    pat_b = mm(filters, to_b)
    for g in range(32):
        for pat, table in ((pat_f, TF), (pat_b, TB)):
            rows = jnp.broadcast_to(pat[g:g + 1], (128, 256))
            skewed = pltpu.roll(rows, 0, 1, stride=1, stride_axis=0)
            table[g // 8, pl.ds((g % 8) * 128, 128), :] = skewed.astype(BF16)


def anti_identity(n):
    r = lax.broadcasted_iota(jnp.int32, (n, n), 0)
    c = lax.broadcasted_iota(jnp.int32, (n, n), 1)
    return jnp.where(r + c == n - 1, 1.0, 0.0).astype(BF16)


def diag(products, rows):
    group = lane_group((rows, products.shape[1]))
    out = products[0:rows]
    for g in range(1, 8):
        out = jnp.where(group == g, products[g * rows:(g + 1) * rows], out)
    return out


def shifted(x, j):
    if j == 0:
        return x
    return pltpu.roll(x, j % x.shape[0], 0)


def compute_chunk(k, U, C, Win, Wout, taps_ref, TF, TB, UT, HID, GP, PART, PSH, PFIL, hook_a, hook_b):
    w = Win[k]
    wo = Wout[k].reshape(128, 512)
    taps = taps_ref[k]
    tf = TF[k]
    tb = TB[k]
    proj, gated, gc, keys, values, queries, ghs = [], [], [], [], [], [], []
    for s in range(2):
        sign = 1 if s == 0 else -1
        kv_at = 0 if s == 0 else 128
        q_at = 128 - kv_at
        pkv = mm(U[s, pl.ds(kv_at, 416), :], w[:, 128:]).astype(BF16)
        pq = mm(U[s, pl.ds(q_at, 416), :], w[:, :128]).astype(BF16)
        gh = mm(C[s], wo, NT).astype(BF16).astype(F32)
        pkv32 = pkv.astype(F32)
        pq32 = pq.astype(F32)
        mkv = jnp.zeros((416, 256), F32)
        mq = jnp.zeros((416, 128), F32)
        for j in range(4):
            mkv = mkv + taps[j:j + 1, 128:] * shifted(pkv32, sign * j)
            mq = mq + taps[j:j + 1, :128] * shifted(pq32, sign * j)
        key, value = mkv[:, :128], mkv[:, 128:]
        gated.append((key * value).astype(BF16))
        keys.append(key)
        values.append(value)
        queries.append(mq)
        ghs.append(gh)
        at = 16 if s == 0 else 0
        gc.append((gh * mq[at:at + 400]).astype(BF16))
        own_kv = 144 if s == 0 else 16
        own_q = 160 - own_kv
        proj.append((pq32[own_q:own_q + 256], pkv32[own_kv:own_kv + 256]))
    hook_a()
    wf = jnp.concatenate([gated[0][:400], gc[1]], axis=1)
    f_parts, b_parts = [], []
    prods = None
    for blk in range(2):
        xf = wf[16 + 128 * blk:272 + 128 * blk]
        f_parts.append(diag(mm(tf, xf), 128))
        xb = jnp.concatenate([gc[0][128 * blk:128 * blk + 256], gated[1][16 + 128 * blk:272 + 128 * blk]], axis=1)
        b_parts.append(diag(mm(tb, xb), 128))
        left = jnp.concatenate([gc[0][128 * blk:128 * blk + 128], gated[1][16 + 128 * blk:144 + 128 * blk]], axis=1)
        left = mm(anti_identity(128), left).astype(BF16)
        group = lane_group((128, 256))
        masked = jnp.concatenate([jnp.where(group == g, left, jnp.zeros_like(left)) for g in range(8)], axis=0)
        term = mm(masked, xf, NT)
        prods = term if prods is None else prods + term
    tf3 = tf.reshape(8, 128, 256)
    tb3 = tb.reshape(8, 128, 256)
    f_last = tf3[:, 112:].reshape(128, 256)
    f_first = tf3[:, :16].reshape(128, 256)
    b_last = tb3[:, 112:].reshape(128, 256)
    b_first = tb3[:, :16].reshape(128, 256)
    conv0_x = diag(mm(f_last, gated[0][160:416]), 16)
    gg1_x = diag(mm(f_first, gc[1][0:256]), 16)
    gg0_x = diag(mm(b_last, gc[0][144:400]), 16)
    conv1_x = diag(mm(b_first, gated[1][0:256]), 16)
    conv = [
        jnp.concatenate([f_parts[0][:, :128], f_parts[1][:, :128], conv0_x], axis=0),
        jnp.concatenate([conv1_x, b_parts[0][:, 128:], b_parts[1][:, 128:]], axis=0),
    ]
    gg = [
        jnp.concatenate([b_parts[0][:, :128], b_parts[1][:, :128], gg0_x], axis=0),
        jnp.concatenate([gg1_x, f_parts[0][:, 128:], f_parts[1][:, 128:]], axis=0),
    ]
    hook_b()
    short = [jnp.zeros((1, 384), F32) for _ in range(4)]
    for s in range(2):
        sign = 1 if s == 0 else -1
        own = 0 if s == 0 else 16
        q_at = 16 if s == 0 else 128
        kv_at = 144 if s == 0 else 0
        gh_at = 0 if s == 0 else 128
        query = queries[s][q_at:q_at + 272]
        hidden = (query[own:own + 256] * conv[s][own:own + 256]).astype(BF16)
        HID[k, pl.ds(256 * s, 256), :] = hidden
        gm = jnp.concatenate(
            [
                ghs[s][gh_at:gh_at + 272] * conv[s],
                gg[s] * values[s][kv_at:kv_at + 272],
                gg[s] * keys[s][kv_at:kv_at + 272],
            ],
            axis=1,
        ).astype(BF16).astype(F32)
        p_own = jnp.concatenate(proj[s], axis=1)
        total = jnp.zeros((256, 384), F32)
        for j in range(4):
            moved = shifted(gm, -sign * j)[own:own + 256]
            total = total + taps[j:j + 1] * moved
            short[j] = short[j] + jnp.sum(p_own * moved, axis=0, keepdims=True)
        GP[k, pl.ds(256 * s, 256), :] = total.astype(BF16)
    PSH[k] = jnp.concatenate(short, axis=0)
    PART[k, :, :, :, pl.ds(0, 384)] = mm(UT[...], GP[k]).reshape(8, 4, 16, 384)
    po = mm(HID[k, pl.ds(0, 256), :], C[0, pl.ds(0, 256), :], TN)
    po = po + mm(HID[k, pl.ds(256, 256), :], C[1, pl.ds(144, 256), :], TN)
    for q in range(4):
        PART[k, :, q, :, pl.ds(384, 128)] = po[:, 128 * q:128 * q + 128].reshape(8, 16, 128)
    rows = []
    for g in range(8):
        r = pltpu.roll(prods[128 * g:128 * g + 128], 129, 1, stride=1, stride_axis=0)
        rows.append(jnp.sum(r, axis=0, keepdims=True))
    PFIL[k] = jnp.concatenate(rows, axis=0)


MESH = pl.DeviceIdType.MESH


def remote(src, dst, send, recv, device):
    copy = pltpu.make_async_remote_copy(
        src_ref=src, dst_ref=dst, send_sem=send, recv_sem=recv, device_id=device, device_id_type=MESH
    )
    copy.start()
    return copy


def wait_bytes(ref, sem):
    pltpu.make_async_copy(ref, ref, sem).wait()


def at_coords(x, y, z, c):
    return ((z // 2) * 4 + x, (z % 2) * 8 + y * 2 + c)


def at_chip(p, c):
    return (p // 8, (p % 8) * 2 + c)


def halves(tile, other):
    lane = lax.broadcasted_iota(jnp.int32, tile.shape, 1)
    low = jnp.where(lane < 64, tile, pltpu.roll(other, 64, 1))
    high = jnp.where(lane < 64, pltpu.roll(tile, 64, 1), other)
    return low, high


def split_cores(wide):
    low, high = [], []
    for t in range(4):
        a, b = halves(wide[:, 256 * t:256 * t + 128], wide[:, 256 * t + 128:256 * t + 256])
        low.append(a)
        high.append(b)
    return jnp.concatenate(low, axis=1), jnp.concatenate(high, axis=1)


def exact_dot(value, zero_one, dims=NN):
    first = value.astype(BF16)
    rest = value - first.astype(F32)
    second = rest.astype(BF16)
    third = (rest - second.astype(F32)).astype(BF16)
    return mm(first, zero_one, dims) + mm(second, zero_one, dims) + mm(third, zero_one, dims)


def block_order():
    row = lax.broadcasted_iota(jnp.int32, (512, 512), 0)
    col = lax.broadcasted_iota(jnp.int32, (512, 512), 1)
    goes = ((row // 16) % 4) * 128 + (row // 64) * 16 + row % 16
    return jnp.where(goes == col, 1.0, 0.0).astype(BF16)


def kernel(
    scale,
    strands_hbm, cotangent_hbm, proj_in_hbm, proj_out_hbm, taps_hbm, filters_hbm,
    out_hbm, grad_hbm, gin_hbm, gout_hbm, gshort_hbm, gfil_hbm,
    strands, cotangent, proj_in, proj_out, taps_in, filters_in,
    out_ref, grad_ref, gin_ref, gout_ref, gshort_ref, gfil_ref,
    U, C, W, WO, WSEND, QM, FLIP, TAPS, TF, TB, UT, HID, GP, PART, PSH, PFIL, OUTP, RP,
    SZ, RZ, SXY, RXY, ZH, FS, FIN, GO,
    SMP, SMZ, SMY, SMYR, SMH, SMX,
    in_sem, out_sem, pair_send, pair_recv, halo_send, halo_recv, fwd_send, fwd_recv,
    w_send, w_recv, wo_send, wo_recv,
    z_send, z_recv, xy_send, xy_recv, zh_send, zh_recv, xg_send, xg_recv, go_send, go_recv,
    sm_send, sm_recv, op_send, op_recv,
):
    arrivals = []
    for i, (src, dst) in enumerate((
        (proj_in_hbm, proj_in), (proj_out_hbm, proj_out), (strands_hbm, strands),
        (cotangent_hbm, cotangent), (taps_hbm, taps_in), (filters_hbm, filters_in),
    )):
        copy = pltpu.make_async_copy(src, dst, in_sem.at[i])
        copy.start()
        arrivals.append(copy)
    departures = []

    def leave(i, src, dst):
        copy = pltpu.make_async_copy(src, dst, out_sem.at[i])
        copy.start()
        departures.append(copy)

    seq, ch = lax.axis_index("seq"), lax.axis_index("ch")
    z_hi, x = seq // 4, seq % 4
    z_lo, y, c = ch // 8, (ch // 2) % 4, ch % 2
    z = z_hi * 2 + z_lo
    b = z_lo * 4 + y
    chip = seq * 8 + b
    before, after = (chip + 127) % 128, (chip + 1) % 128
    partner = at_coords(x, y, z, 1 - c)
    z_above, z_below = (z + 1) % 8, (z + 7) % 8
    z_up, z_down = at_coords(x, y, z_above, c), at_coords(x, y, z_below, c)
    is_first = c == 0

    barrier = pltpu.get_barrier_semaphore()
    peers = [partner]
    for zz in (z_above, z_below):
        for cc in (0, 1):
            peers.append(at_coords(x, y, zz, cc))
    for dx in range(4):
        for dy in range(4):
            if dx or dy:
                peers.append(at_coords((x + dx) % 4, (y + dy) % 4, z, c))
    for d in range(1, 4):
        peers.append(at_coords(x, y, (z + 2 * d) % 8, c))
        peers.append(at_coords((x + d) % 4, y, z, 1 - c))
        peers.append(at_coords(x, (y + d) % 4, z, 1 - c))
    for q in (before, after):
        peers.append(at_chip(q, 0))
        peers.append(at_chip(q, 1))
    for peer in peers:
        pl.semaphore_signal(barrier, inc=1, device_id=peer, device_id_type=MESH)

    QM[...] = block_order()
    FLIP[...] = anti_identity(512)
    my_rows = pl.multiple_of(64 * b + 32 * c, 32)
    arrivals[0].wait()
    low, high = [], []
    for s in range(3):
        a, o = split_cores(proj_in[:, pl.ds(s * 1024, 1024)].astype(F32))
        low.append(a)
        high.append(o)
    moved = mm(jnp.concatenate(low + high, axis=0).astype(BF16), QM[...])
    for k in range(4):
        for s in range(3):
            lanes = pl.ds(128 * s, 128)
            even = moved[32 * s:32 * s + 32, 128 * k:128 * k + 128]
            odd = moved[96 + 32 * s:128 + 32 * s, 128 * k:128 * k + 128]
            W[k, pl.ds(my_rows, 32), lanes] = jnp.where(is_first, even, odd).astype(BF16)
            WSEND[k, :, lanes] = jnp.where(is_first, odd, even).astype(BF16)
    arrivals[1].wait()
    for k in range(4):
        WO[k, b] = proj_out[pl.ds(16 * k, 16), :]
    own = pl.multiple_of(144 + 128 * c, 16)
    own_c0 = pl.multiple_of(128 * c, 16)
    arrivals[2].wait()
    U[0, pl.ds(own, 128), :] = strands[0]
    U[1, pl.ds(own, 128), :] = mm(strands[1], FLIP[...]).astype(BF16)
    arrivals[3].wait()
    C[0, pl.ds(own_c0, 128), :] = cotangent[0]
    C[1, pl.ds(own, 128), :] = mm(cotangent[1], FLIP[...]).astype(BF16)
    arrivals[4].wait()
    arrivals[5].wait()
    pl.semaphore_wait(barrier, len(peers))

    def wo_half(m, bb, half):
        return WO.at[m, bb, :, pl.ds(256 * half, 256)]

    def w_half(m, bb, half):
        return W.at[m, pl.ds(pl.multiple_of(64 * bb + 32 * half, 32), 32), :]

    def gather_first(m):
        mine = W.at[m, pl.ds(my_rows, 32), :]
        theirs = WSEND.at[m]
        place = W.at[m, pl.ds(my_rows, 32), :]
        remote(theirs, place, w_send.at[m], w_recv.at[m, 0], partner)
        for d in (1, 3, 2):
            yy = (y + d) % 4
            remote(mine, place, w_send.at[m], w_recv.at[m, 0], at_coords(x, yy, z, c))
            remote(theirs, place, w_send.at[m], w_recv.at[m, 0], at_coords(x, yy, z, 1 - c))
            remote(WO.at[m, b], WO.at[m, b], wo_send.at[m], wo_recv.at[m, 0], at_coords(x, yy, z, c))
        z_side = jnp.where(is_first, z_above, z_below)
        remote(mine, place, w_send.at[m], w_recv.at[m, 1], at_coords(x, y, z_side, c))
        remote(theirs, place, w_send.at[m], w_recv.at[m, 1], at_coords(x, y, z_side, 1 - c))
        for half, side in ((0, z_up), (1, z_down)):
            remote(wo_half(m, b, half), wo_half(m, b, half), wo_send.at[m], wo_recv.at[m, 1], side)

    def gather_second(m):
        wait_bytes(W.at[m, pl.ds(0, 224), :], w_recv.at[m, 0])
        wait_bytes(WO.at[m, pl.ds(0, 3)], wo_recv.at[m, 0])
        for d in (1, 3, 2):
            bb = z_lo * 4 + (y + d) % 4
            for half, side in ((0, z_up), (1, z_down)):
                remote(w_half(m, bb, half), w_half(m, bb, half), w_send.at[m], w_recv.at[m, 1], side)
                remote(wo_half(m, bb, half), wo_half(m, bb, half), wo_send.at[m], wo_recv.at[m, 1], side)

    def gather_last(m):
        wait_bytes(W.at[m, pl.ds(0, 256), :], w_recv.at[m, 1])
        wait_bytes(WO.at[m, pl.ds(0, 4)], wo_recv.at[m, 1])

    def gather_sent(m):
        wait_bytes(W.at[m, pl.ds(0, 480), :], w_send.at[m])
        wait_bytes(WO.at[m, pl.ds(0, 7)], wo_send.at[m])

    gather_first(0)

    far = jnp.where(is_first, before, after)
    near = jnp.where(is_first, after, before)
    big_at = pl.multiple_of(jnp.where(is_first, 400, 16), 16)
    small_src = pl.multiple_of(own + jnp.where(is_first, 112, 0), 16)
    small_at = pl.multiple_of(jnp.where(is_first, 0, 528), 16)
    halo = []
    for s in range(2):
        halo.append(remote(
            U.at[s, pl.ds(own, 128), :], U.at[s, pl.ds(big_at, 128), :],
            halo_send.at[s], halo_recv.at[1 - c], at_chip(far, s)))
        halo.append(remote(
            U.at[s, pl.ds(small_src, 16), :], U.at[s, pl.ds(small_at, 16), :],
            halo_send.at[2 + s], halo_recv.at[2 + c], at_chip(near, s)))
    c_own = pl.multiple_of(jnp.where(is_first, 0, 272), 16)
    c_big = pl.multiple_of(jnp.where(is_first, 256, 16), 16)
    halo.append(remote(
        C.at[c, pl.ds(c_own, 128), :], C.at[c, pl.ds(c_big, 128), :],
        halo_send.at[4], halo_recv.at[4], at_chip(far, c)))
    c_small_src = pl.multiple_of(jnp.where(is_first, 144 + 112, 128), 16)
    c_small = pl.multiple_of(jnp.where(is_first, 0, 384), 16)
    halo.append(remote(
        C.at[1 - c, pl.ds(c_small_src, 16), :], C.at[1 - c, pl.ds(c_small, 16), :],
        halo_send.at[5], halo_recv.at[5], at_chip(near, 1 - c)))
    pair = [
        remote(U.at[s, pl.ds(own, 128), :], U.at[s, pl.ds(own, 128), :], pair_send.at[s], pair_recv.at[s], partner)
        for s in range(2)
    ]
    pair.append(remote(
        C.at[0, pl.ds(own_c0, 128), :], C.at[0, pl.ds(own_c0, 128), :], pair_send.at[2], pair_recv.at[2], partner))
    pair.append(remote(
        C.at[1, pl.ds(own, 128), :], C.at[1, pl.ds(own, 128), :], pair_send.at[3], pair_recv.at[3], partner))
    for m in range(1, 4):
        gather_first(m)

    picked = []
    for s in range(3):
        a, o = split_cores(taps_in[:, pl.ds(s * 1024, 1024)])
        picked.append(jnp.where(is_first, a, o))
    picked = exact_dot(jnp.concatenate(picked, axis=0), QM[...])
    for k in range(4):
        for s in range(3):
            TAPS[k, :, pl.ds(128 * s, 128)] = picked[4 * s:4 * s + 4, 128 * k:128 * k + 128]
    row = lax.broadcasted_iota(jnp.int32, (32, 64), 0)
    col = lax.broadcasted_iota(jnp.int32, (32, 64), 1)
    chosen = jnp.where((row % 8) * 8 + 4 * c + row // 8 == col, 1.0, 0.0).astype(BF16)
    build_tables(mm(chosen, filters_in[...]).astype(BF16), TF, TB)

    gather_second(0)
    wait_bytes(U.at[c, pl.ds(16, 128), :], halo_recv.at[0])
    wait_bytes(U.at[c, pl.ds(400, 128), :], halo_recv.at[1])
    wait_bytes(U.at[c, pl.ds(0, 16), :], halo_recv.at[2])
    wait_bytes(U.at[c, pl.ds(528, 16), :], halo_recv.at[3])
    wait_bytes(C.at[c, pl.ds(c_big, 128), :], halo_recv.at[4])
    wait_bytes(C.at[c, pl.ds(pl.multiple_of(jnp.where(is_first, 384, 0), 16), 16), :], halo_recv.at[5])
    c_halo = pl.multiple_of(jnp.where(is_first, 256, 0), 16)
    c_halo_other = pl.multiple_of(jnp.where(is_first, 0, 256), 16)
    fwd = []
    for i, at in enumerate((0, 400)):
        rows = U.at[c, pl.ds(at, 144), :]
        fwd.append(remote(rows, rows, fwd_send.at[i], fwd_recv.at[i], partner))
    rows = C.at[c, pl.ds(c_halo, 144), :]
    fwd.append(remote(rows, rows, fwd_send.at[2], fwd_recv.at[2], partner))
    for copy in pair:
        copy.wait_recv()
    for s in range(2):
        UT[:, pl.ds(256 * s, 256)] = jnp.transpose(U[s, pl.ds(144, 256), :])
    gather_second(1)
    for i, at in enumerate((0, 400)):
        wait_bytes(U.at[1 - c, pl.ds(at, 144), :], fwd_recv.at[i])
    wait_bytes(C.at[1 - c, pl.ds(c_halo_other, 144), :], fwd_recv.at[2])
    for copy in fwd:
        copy.wait_send()

    @pl.when(chip == 0)
    def _():
        U[:, pl.ds(0, 144), :] = jnp.zeros((2, 144, 512), BF16)
        C[1, pl.ds(0, 144), :] = jnp.zeros((144, 512), BF16)

    @pl.when(chip == 127)
    def _():
        U[:, pl.ds(400, 144), :] = jnp.zeros((2, 144, 512), BF16)
        C[0, pl.ds(256, 144), :] = jnp.zeros((144, 512), BF16)

    def z_start(k):
        SZ[k] = PART[k, pl.ds((1 - z_lo) * 4, 4)].astype(BF16)
        remote(SZ.at[k, :, pl.ds(0, 2)], RZ.at[k, :, pl.ds(0, 2)], z_send.at[k], z_recv.at[k, 0], z_up)
        remote(SZ.at[k, :, pl.ds(2, 2)], RZ.at[k, :, pl.ds(2, 2)], z_send.at[k], z_recv.at[k, 1], z_down)

    def xy_start(k):
        wait_bytes(RZ.at[k, :, pl.ds(0, 2)], z_recv.at[k, 0])
        wait_bytes(RZ.at[k, :, pl.ds(2, 2)], z_recv.at[k, 1])
        SXY[k] = (PART[k, pl.ds(z_lo * 4, 4)] + RZ[k].astype(F32)).astype(BF16)
        for dx in range(4):
            for dy in range(4):
                if dx or dy:
                    xx, yy = (x + dx) % 4, (y + dy) % 4
                    remote(SXY.at[k, yy, xx], RXY.at[k, 4 * dx + dy - 1],
                           xy_send.at[k], xy_recv.at[k], at_coords(xx, yy, z, c))

    def zh_start(k):
        wait_bytes(RXY.at[k], xy_recv.at[k])
        total = SXY[k, y, x].astype(F32)
        for i in range(15):
            total = total + RXY[k, i].astype(F32)
        ZH[k, z_hi] = total.astype(BF16)
        for d in range(1, 4):
            remote(ZH.at[k, z_hi], ZH.at[k, z_hi], zh_send.at[k], zh_recv.at[k], at_coords(x, y, (z + 2 * d) % 8, c))

    target = x // 2
    row_at = pl.multiple_of(16 * (x % 2), 16)
    go_at = pl.multiple_of(128 * x, 128)

    def xg_start(k):
        wait_bytes(ZH.at[k, pl.ds(0, 3)], zh_recv.at[k])
        total = ZH[k, 0].astype(F32)
        for i in range(1, 4):
            total = total + ZH[k, i].astype(F32)
        FS[k] = total.astype(BF16)
        part = FS.at[k, :, pl.ds(0, 384)]
        place = FIN.at[k, c, pl.ds(row_at, 16), :]
        piece = FS.at[k, :, pl.ds(384, 128)]
        spot = GO.at[k, :, pl.ds(go_at, 128)]
        for d in range(1, 4):
            remote(part, place, xg_send.at[k], xg_recv.at[k], at_coords((x + d) % 4, y, z, target))
            remote(piece, spot, go_send.at[k], go_recv.at[k], at_coords((x + d) % 4, y, z, c))

        @pl.when(c == target)
        def _():
            pltpu.make_async_copy(part, place, xg_recv.at[k]).start()

        @pl.when(c != target)
        def _():
            remote(part, place, xg_send.at[k], xg_recv.at[k], partner)

        GO[k, :, pl.ds(go_at, 128)] = FS[k, :, pl.ds(384, 128)]

    def reduced(k):
        wait_bytes(FIN.at[k], xg_recv.at[k])
        wait_bytes(GO.at[k, :, pl.ds(0, 384)], go_recv.at[k])

    def reduce_sent(k):
        wait_bytes(SZ.at[k], z_send.at[k])
        wait_bytes(RXY.at[k], xy_send.at[k])
        wait_bytes(ZH.at[k, pl.ds(0, 3)], zh_send.at[k])
        wait_bytes(FS.at[pl.ds(0, 3), :, pl.ds(0, 384)], xg_send.at[k])
        wait_bytes(FS.at[pl.ds(0, 3), :, pl.ds(384, 128)], go_send.at[k])

        @pl.when(c != target)
        def _():
            wait_bytes(FS.at[k, :, pl.ds(0, 384)], xg_send.at[k])

    def small_z():
        taps_rows = []
        for k in range(4):
            taps_rows.append(jnp.concatenate(
                [PSH[k, :, pl.ds(128 * s, 128)] for s in range(3)], axis=0))
        back = exact_dot(jnp.concatenate(taps_rows, axis=1), QM[...], NT)
        fil = [pltpu.roll(PFIL[k], 255, 1)[:, :128] for k in range(4)]
        for i in range(8):
            m = i // 2
            tiles = (3 * m, 3 * m + 1) if i % 2 == 0 else (3 * m + 1, 3 * m + 2)
            rows = []
            for t in tiles:
                s, p = t // 4, t % 4
                rows.append(back[4 * s:4 * s + 4, 128 * p:128 * p + 128])
            rows += [fil[k][i:i + 1] for k in range(4)]
            SMP[i] = jnp.concatenate(rows + [jnp.zeros((4, 128), F32)], axis=0)
        remote(SMP.at[pl.ds((1 - z_lo) * 4, 4)], SMZ, sm_send.at[0], sm_recv.at[0], z_up)

    def small_y():
        wait_bytes(SMZ, sm_recv.at[0])
        SMY[...] = SMP[pl.ds(z_lo * 4, 4)] + SMZ[...]
        for d in range(1, 4):
            yy = (y + d) % 4
            remote(SMY.at[yy], SMYR.at[d - 1], sm_send.at[1], sm_recv.at[1], at_coords(x, yy, z, c))

    def small_h():
        wait_bytes(SMYR, sm_recv.at[1])
        SMH[z_hi] = SMY[y] + SMYR[0] + SMYR[1] + SMYR[2]
        for d in range(1, 4):
            remote(SMH.at[z_hi], SMH.at[z_hi], sm_send.at[2], sm_recv.at[2], at_coords(x, y, (z + 2 * d) % 8, c))

    def small_x():
        wait_bytes(SMH.at[pl.ds(0, 3)], sm_recv.at[2])
        SMX[c, x] = SMH[0] + SMH[1] + SMH[2] + SMH[3]
        for d in range(1, 4):
            for cc in (c, 1 - c):
                remote(SMX.at[c, x], SMX.at[c, x], sm_send.at[3], sm_recv.at[3], at_coords((x + d) % 4, y, z, cc))
        remote(SMX.at[c, x], SMX.at[c, x], sm_send.at[3], sm_recv.at[3], partner)

    def small_last():
        wait_bytes(SMP.at[pl.ds(0, 7)], sm_recv.at[3])
        e = SMX[0, 0] + SMX[0, 1] + SMX[0, 2] + SMX[0, 3]
        o = SMX[1, 0] + SMX[1, 1] + SMX[1, 2] + SMX[1, 3]
        mine = jnp.where(is_first, e, o)
        gfil_ref[...] = exact_dot(mine, anti_identity(128))[8:12] * scale
        lane = lax.broadcasted_iota(jnp.int32, (4, 128), 1)

        def blocks(v):
            a, t = v[0:4], v[4:8]
            turned_a, turned_t = pltpu.roll(a, 64, 1), pltpu.roll(t, 64, 1)
            even = b % 2 == 0
            return (
                jnp.where(even, a, turned_a),
                jnp.where(even, turned_a, t),
                jnp.where(even, t, turned_t),
            )

        e, o = blocks(e), blocks(o)
        one = jnp.where(is_first, e[0], o[1])
        two = jnp.where(is_first, o[0], e[2])
        three = jnp.where(is_first, e[1], o[2])
        gshort_ref[:, pl.ds(0, 128)] = jnp.where(lane < 64, one, pltpu.roll(two, 64, 1)) * scale
        gshort_ref[:, pl.ds(128, 64)] = three[:, :64] * scale

    def small_sent():
        wait_bytes(SMZ, sm_send.at[0])
        wait_bytes(SMYR, sm_send.at[1])
        wait_bytes(SMYR, sm_send.at[2])
        wait_bytes(SMP.at[pl.ds(0, 7)], sm_send.at[3])


    def body(k, carry):
        gather_last(k)

        def hook_a():
            @pl.when(k == 0)
            def _():
                gather_second(2)

        def hook_b():
            @pl.when(k == 0)
            def _():
                gather_second(3)

        compute_chunk(k, U, C, W, WO, TAPS, TF, TB, UT, HID, GP, PART, PSH, PFIL, hook_a, hook_b)
        z_start(k)

        @pl.when(k >= 1)
        def _():
            xy_start(k - 1)

        @pl.when(k >= 2)
        def _():
            zh_start(k - 2)

        @pl.when(k >= 3)
        def _():
            xg_start(k - 3)

        return carry

    lax.fori_loop(0, 4, body, 0)

    small_z()
    other_rows = 128 * (1 - c)
    op = []
    for o in range(2):
        if o == 0:
            res = mm(HID[0], WO[0].reshape(128, 512))
            for k in range(1, 4):
                res = res + mm(HID[k], WO[k].reshape(128, 512))
        else:
            res = mm(GP[0], W[0], NT)
            for k in range(1, 4):
                res = res + mm(GP[k], W[k], NT)
        OUTP[o] = res
        for s in range(2):
            rows = pl.ds(pl.multiple_of(256 * s + other_rows, 128), 128)
            op.append(remote(OUTP.at[o, rows, :], RP.at[o, s], op_send.at[o, s], op_recv.at[o, s], partner))
    xy_start(3)
    small_y()
    for o, (ref, hbm) in enumerate(((out_ref, out_hbm), (grad_ref, grad_hbm))):
        for s in range(2):
            op[2 * o + s].wait_recv()
            rows = pl.ds(pl.multiple_of(256 * s + 128 * c, 128), 128)
            value = (OUTP[o, rows, :] + RP[o, s]).astype(BF16)
            ref[s] = value if s == 0 else mm(value, FLIP[...]).astype(BF16)
        leave(o, ref, hbm)
    zh_start(2)
    xg_start(1)
    small_h()
    zh_start(3)
    xg_start(2)
    small_x()
    xg_start(3)
    for copy in pair + halo + op:
        copy.wait_send()
    for m in range(4):
        gather_sent(m)
    small_last()
    leave(4, gshort_ref, gshort_hbm)
    leave(5, gfil_ref, gfil_hbm)
    for k in range(4):
        reduced(k)
    for k in range(4):
        gout_ref[pl.ds(16 * k, 16), :] = GO[k].astype(F32) * scale
    leave(3, gout_ref, gout_hbm)
    rows = []
    for cc in range(2):
        for s in range(3):
            rows.append(jnp.concatenate([FIN[k, cc, :, pl.ds(128 * s, 128)] for k in range(4)], axis=1))
    back = mm(jnp.concatenate(rows, axis=0), QM[...], NT) * scale
    for s in range(3):
        for t in range(4):
            lanes = slice(128 * t, 128 * t + 128)
            first, second = halves(back[32 * s:32 * s + 32, lanes], back[96 + 32 * s:128 + 32 * s, lanes])
            gin_ref[:, pl.ds(s * 1024 + t * 256, 128)] = first
            gin_ref[:, pl.ds(s * 1024 + t * 256 + 128, 128)] = second
    leave(2, gin_ref, gin_hbm)
    for k in range(4):
        reduce_sent(k)
    small_sent()
    for copy in departures:
        copy.wait()


def hand_over(*refs):
    n = 6
    sources, targets, held = refs[:n], refs[n:2 * n], refs[2 * n:3 * n]
    in_sem, out_sem = refs[3 * n:]
    arrive = [pltpu.make_async_copy(sources[i], held[i], in_sem.at[i]) for i in range(n)]
    leave = [pltpu.make_async_copy(held[i], targets[i], out_sem.at[i]) for i in range(n)]
    for copy in arrive:
        copy.start()
    for i in range(n):
        arrive[i].wait()
        leave[i].start()
    for copy in leave:
        copy.wait()


def shards(strands, cotangent, proj_in, proj_out, short_taps, filters):
    length = strands.shape[1] * lax.axis_size(("seq", "ch"))
    scale = float(length) ** (-0.5)
    dma = pltpu.SemaphoreType.DMA
    outs = (
        jax.ShapeDtypeStruct((2, 128, 512), BF16),
        jax.ShapeDtypeStruct((2, 128, 512), BF16),
        jax.ShapeDtypeStruct((32, 3072), F32),
        jax.ShapeDtypeStruct((64, 512), F32),
        jax.ShapeDtypeStruct((4, 192), F32),
        jax.ShapeDtypeStruct((4, 128), F32),
    )
    scratch = [
        pltpu.VMEM((2, 128, 512), BF16),
        pltpu.VMEM((2, 128, 512), BF16),
        pltpu.VMEM((32, 3072), BF16),
        pltpu.VMEM((64, 512), BF16),
        pltpu.VMEM((4, 3072), F32),
        pltpu.VMEM((64, 128), BF16),
    ]
    scratch += [pltpu.VMEM(o.shape, o.dtype) for o in outs]
    scratch += [
        pltpu.VMEM((2, 544, 512), BF16),
        pltpu.VMEM((2, 400, 512), BF16),
        pltpu.VMEM((4, 512, 384), BF16),
        pltpu.VMEM((4, 8, 16, 512), BF16),
        pltpu.VMEM((4, 32, 384), BF16),
        pltpu.VMEM((512, 512), BF16),
        pltpu.VMEM((512, 512), BF16),
        pltpu.VMEM((4, 4, 384), F32),
        pltpu.VMEM((4, 1024, 256), BF16),
        pltpu.VMEM((4, 1024, 256), BF16),
        pltpu.VMEM((512, 512), BF16),
        pltpu.VMEM((4, 512, 128), BF16),
        pltpu.VMEM((4, 512, 384), BF16),
        pltpu.VMEM((4, 8, 4, 16, 512), F32),
        pltpu.VMEM((4, 4, 384), F32),
        pltpu.VMEM((4, 8, 256), F32),
        pltpu.VMEM((2, 512, 512), F32),
        pltpu.VMEM((2, 2, 128, 512), F32),
        pltpu.VMEM((4, 4, 4, 16, 512), BF16),
        pltpu.VMEM((4, 4, 4, 16, 512), BF16),
        pltpu.VMEM((4, 4, 4, 16, 512), BF16),
        pltpu.VMEM((4, 15, 16, 512), BF16),
        pltpu.VMEM((4, 4, 16, 512), BF16),
        pltpu.VMEM((4, 16, 512), BF16),
        pltpu.VMEM((4, 2, 32, 384), BF16),
        pltpu.VMEM((4, 16, 512), BF16),
        pltpu.VMEM((8, 16, 128), F32),
        pltpu.VMEM((4, 16, 128), F32),
        pltpu.VMEM((4, 16, 128), F32),
        pltpu.VMEM((3, 16, 128), F32),
        pltpu.VMEM((4, 16, 128), F32),
        pltpu.VMEM((2, 4, 16, 128), F32),
    ]
    scratch += [
        dma((6,)), dma((6,)), dma((4,)), dma((4,)), dma((6,)), dma((6,)), dma((3,)), dma((3,)),
        dma((4,)), dma((4, 2)), dma((4,)), dma((4, 2)),
        dma((4,)), dma((4, 2)), dma((4,)), dma((4,)), dma((4,)), dma((4,)), dma((4,)), dma((4,)), dma((4,)), dma((4,)),
        dma((4,)), dma((4,)), dma((2, 2)), dma((2, 2)),
    ]
    anywhere = pl.BlockSpec(memory_space=pl.ANY)
    results = pl.pallas_call(
        functools.partial(kernel, scale),
        out_shape=outs,
        in_specs=[anywhere] * 6,
        out_specs=tuple([anywhere] * 6),
        scratch_shapes=scratch,
        compiler_params=pltpu.CompilerParams(
            collective_id=0, has_side_effects=True, vmem_limit_bytes=58 * 2**20
        ),
        cost_estimate=pl.CostEstimate(flops=9 * 10**9, bytes_accessed=4 * 10**6, transcendentals=0),
    )(strands, cotangent, proj_in, proj_out, short_taps.T, filters)
    results = pl.pallas_call(
        hand_over,
        out_shape=outs,
        in_specs=[anywhere] * 6,
        out_specs=tuple([anywhere] * 6),
        scratch_shapes=[pltpu.VMEM(o.shape, o.dtype) for o in outs] + [dma((6,)), dma((6,))],
    )(*results)
    return results[:4] + (results[4].T, results[5])


def solution(mesh):
    placed = P(None, ("seq", "ch"), None)
    rows = P("ch", None)
    return jax.shard_map(
        shards,
        mesh=mesh,
        in_specs=(placed, placed, rows, rows, P(), P()),
        out_specs=(placed, placed, rows, rows, rows, rows),
        check_vma=False,
    )
```

```python
import functools

import jax
import jax.numpy as jnp
from jax import lax
from jax.experimental import pallas as pl
from jax.experimental.pallas import tpu as pltpu
from jax.sharding import PartitionSpec as P

F32 = jnp.float32
BF16 = jnp.bfloat16
NN = (((1,), (0,)), ((), ()))
NT = (((1,), (1,)), ((), ()))
TN = (((0,), (0,)), ((), ()))


def mm(a, b, dims=NN):
    return lax.dot_general(a, b, dims, preferred_element_type=F32)


def lane_group(shape, span):
    return (lax.broadcasted_iota(jnp.int32, shape, 1) % span) // 16


def halves(tile, other):
    lane = lax.broadcasted_iota(jnp.int32, tile.shape, 1)
    low = jnp.where(lane < 64, tile, pltpu.roll(other, 64, 1))
    high = jnp.where(lane < 64, pltpu.roll(tile, 64, 1), other)
    return low, high


def build_tables(filters, TF, TB):
    t = lax.broadcasted_iota(jnp.int32, (128, 256), 0)
    k = lax.broadcasted_iota(jnp.int32, (128, 256), 1)
    to_f = jnp.where(t + k == 128, 1.0, 0.0).astype(BF16)
    to_b = jnp.where(t == k, 1.0, 0.0).astype(BF16)
    pat_f = mm(filters, to_f)
    pat_b = mm(filters, to_b)
    for g in range(32):
        for pat, table in ((pat_f, TF), (pat_b, TB)):
            rows = jnp.broadcast_to(pat[g:g + 1], (128, 256))
            skewed = pltpu.roll(rows, 0, 1, stride=1, stride_axis=0)
            table[g // 8, pl.ds((g % 8) * 128, 128), :] = skewed.astype(BF16)


def anti_identity(n):
    r = lax.broadcasted_iota(jnp.int32, (n, n), 0)
    c = lax.broadcasted_iota(jnp.int32, (n, n), 1)
    return jnp.where(r + c == n - 1, 1.0, 0.0).astype(BF16)


def diag(products, rows, count):
    group = lane_group((rows, products.shape[1]), 16 * count)
    out = products[0:rows]
    for g in range(1, count):
        out = jnp.where(group == g, products[g * rows:(g + 1) * rows], out)
    return out


def compute_chunk(k, U, C, Win, Wout, taps_ref, TF, TB, UT, HID, GP, PART, PSH, PFIL, ROWS, hook_a, hook_b):
    w = Win[k]
    wo = Wout[k].reshape(128, 512)
    taps = taps_ref[k]
    tf = TF[k]
    tb = TB[k]
    own_proj, gated, gc, keys, values, queries, ghs = [], [], [], [], [], [], []
    for s in range(2):
        sign = 1 if s == 0 else -1
        kv_at = 0 if s == 0 else 128
        q_at = 128 - kv_at
        pkv = mm(U[s, pl.ds(kv_at, 416), :], w[:, 128:]).astype(BF16)
        pq = mm(U[s, pl.ds(q_at, 416), :], w[:, :128]).astype(BF16)
        gh = mm(C[s], wo, NT).astype(BF16).astype(F32)
        mixed = []
        own_kv = 144 if s == 0 else 16
        own_q = 160 - own_kv
        for part, values_in in enumerate((pq, pkv[:, :128], pkv[:, 128:])):
            held = ROWS.at[3 * s + part]
            wide = values_in.astype(F32)
            held[pl.ds(8, 416), :] = wide
            t = taps[:, 128 * part:128 * part + 128]
            total = t[0:1] * wide
            for j in range(1, 4):
                total = total + t[j:j + 1] * held[pl.ds(8 - sign * j, 416), :]
            mixed.append(total)
        mq, key, value = mixed
        own_proj.append((own_q, own_kv, own_kv))
        gated.append((key * value).astype(BF16))
        keys.append(key)
        values.append(value)
        queries.append(mq)
        ghs.append(gh)
        at = 16 if s == 0 else 0
        gc.append((gh * mq[at:at + 400]).astype(BF16))
    hook_a()
    def packed(first, second):
        low_first, high_first = halves(*first)
        low_second, high_second = halves(*second)
        return (
            jnp.concatenate([low_first, low_second], axis=1),
            jnp.concatenate([high_first, high_second], axis=1),
        )

    def blocks_of(value, at, rows):
        return value[at:at + rows], value[at + 128:at + 128 + rows]

    xf = packed(blocks_of(gated[0], 16, 256), blocks_of(gc[1], 16, 256))
    xb = packed(blocks_of(gc[0], 0, 256), blocks_of(gated[1], 16, 256))
    left = packed(blocks_of(gc[0], 0, 128), blocks_of(gated[1], 16, 128))
    reverse = anti_identity(128)
    group = lane_group((128, 256), 64)
    yf, yb, prods = [], [], []
    for h in range(2):
        yf.append(diag(mm(tf[512 * h:512 * h + 512], xf[h]), 128, 4))
        yb.append(diag(mm(tb[512 * h:512 * h + 512], xb[h]), 128, 4))
        turned = mm(reverse, left[h]).astype(BF16)
        masked = jnp.concatenate([jnp.where(group == g, turned, jnp.zeros_like(turned)) for g in range(4)], axis=0)
        prods.append(mm(masked, xf[h], NT))
    f_first_strand = halves(yf[0][:, :128], yf[1][:, :128])
    f_second_strand = halves(yf[0][:, 128:], yf[1][:, 128:])
    b_first_strand = halves(yb[0][:, :128], yb[1][:, :128])
    b_second_strand = halves(yb[0][:, 128:], yb[1][:, 128:])
    tf3 = tf.reshape(8, 128, 256)
    tb3 = tb.reshape(8, 128, 256)
    f_last = tf3[:, 112:].reshape(128, 256)
    f_first = tf3[:, :16].reshape(128, 256)
    b_last = tb3[:, 112:].reshape(128, 256)
    b_first = tb3[:, :16].reshape(128, 256)
    conv0_x = diag(mm(f_last, gated[0][160:416]), 16, 8)
    gg1_x = diag(mm(f_first, gc[1][0:256]), 16, 8)
    gg0_x = diag(mm(b_last, gc[0][144:400]), 16, 8)
    conv1_x = diag(mm(b_first, gated[1][0:256]), 16, 8)
    conv = [
        jnp.concatenate([*f_first_strand, conv0_x], axis=0),
        jnp.concatenate([conv1_x, *b_second_strand], axis=0),
    ]
    gg = [
        jnp.concatenate([*b_first_strand, gg0_x], axis=0),
        jnp.concatenate([gg1_x, *f_second_strand], axis=0),
    ]
    hook_b()
    short = [[None] * 3 for _ in range(4)]
    for s in range(2):
        sign = 1 if s == 0 else -1
        own = 0 if s == 0 else 16
        q_at = 16 if s == 0 else 128
        kv_at = 144 if s == 0 else 0
        gh_at = 0 if s == 0 else 128
        query = queries[s][q_at:q_at + 272]
        hidden = (query[own:own + 256] * conv[s][own:own + 256]).astype(BF16)
        HID[k, pl.ds(256 * s, 256), :] = hidden
        grads = (
            ghs[s][gh_at:gh_at + 272] * conv[s],
            gg[s] * values[s][kv_at:kv_at + 272],
            gg[s] * keys[s][kv_at:kv_at + 272],
        )
        for part in range(3):
            held = ROWS.at[6 + 3 * s + part]
            p_own = ROWS[3 * s + part, pl.ds(8 + own_proj[s][part], 256), :]
            gm = grads[part].astype(BF16).astype(F32)
            held[pl.ds(8, 272), :] = gm
            t = taps[:, 128 * part:128 * part + 128]
            total = None
            for j in range(4):
                moved = gm[own:own + 256] if j == 0 else held[pl.ds(8 + own + sign * j, 256), :]
                term = t[j:j + 1] * moved
                total = term if total is None else total + term
                column = jnp.sum(p_own * moved, axis=0, keepdims=True)
                short[j][part] = column if s == 0 else short[j][part] + column
            GP[k, pl.ds(256 * s, 256), pl.ds(128 * part, 128)] = total.astype(BF16)
    for j in range(4):
        for part in range(3):
            PSH[k, pl.ds(j, 1), pl.ds(128 * part, 128)] = short[j][part]
    PART[k, :, :, :, pl.ds(0, 384)] = mm(UT[...], GP[k]).reshape(8, 4, 16, 384)
    po = mm(HID[k, pl.ds(0, 256), :], C[0, pl.ds(0, 256), :], TN)
    po = po + mm(HID[k, pl.ds(256, 256), :], C[1, pl.ds(144, 256), :], TN)
    for q in range(4):
        PART[k, :, q, :, pl.ds(384, 128)] = po[:, 128 * q:128 * q + 128].reshape(8, 16, 128)
    rows = []
    for g in range(8):
        r = pltpu.roll(prods[g // 4][128 * (g % 4):128 * (g % 4) + 128], 129, 1, stride=1, stride_axis=0)
        rows.append(jnp.sum(r, axis=0, keepdims=True))
    PFIL[k] = jnp.concatenate(rows, axis=0)


MESH = pl.DeviceIdType.MESH


def remote(src, dst, send, recv, device):
    copy = pltpu.make_async_remote_copy(
        src_ref=src, dst_ref=dst, send_sem=send, recv_sem=recv, device_id=device, device_id_type=MESH
    )
    copy.start()
    return copy


def wait_bytes(ref, sem):
    pltpu.make_async_copy(ref, ref, sem).wait()


def at_coords(x, y, z, c):
    return ((z // 2) * 4 + x, (z % 2) * 8 + y * 2 + c)


def at_chip(p, c):
    return (p // 8, (p % 8) * 2 + c)


def split_cores(wide):
    low, high = [], []
    for t in range(4):
        a, b = halves(wide[:, 256 * t:256 * t + 128], wide[:, 256 * t + 128:256 * t + 256])
        low.append(a)
        high.append(b)
    return jnp.concatenate(low, axis=1), jnp.concatenate(high, axis=1)


def exact_dot(value, zero_one, dims=NN):
    first = value.astype(BF16)
    rest = value - first.astype(F32)
    second = rest.astype(BF16)
    third = (rest - second.astype(F32)).astype(BF16)
    return mm(first, zero_one, dims) + mm(second, zero_one, dims) + mm(third, zero_one, dims)


def block_order():
    row = lax.broadcasted_iota(jnp.int32, (512, 512), 0)
    col = lax.broadcasted_iota(jnp.int32, (512, 512), 1)
    goes = ((row // 16) % 4) * 128 + (row // 64) * 16 + row % 16
    return jnp.where(goes == col, 1.0, 0.0).astype(BF16)


def kernel(
    scale,
    strands_hbm, cotangent_hbm, proj_in_hbm, proj_out_hbm, taps_hbm, filters_hbm,
    out_hbm, grad_hbm, gin_hbm, gout_hbm, gshort_hbm, gfil_hbm,
    strands, cotangent, proj_in, proj_out, taps_in, filters_in,
    out_ref, grad_ref, gin_ref, gout_ref, gshort_ref, gfil_ref,
    U, C, W, WO, WSEND, QM, FLIP, TAPS, TF, TB, UT, HID, GP, PART, PSH, PFIL, ROWS, OUTP, RP,
    SZ, RZ, SXY, RXY, ZH, FS, FIN, GO,
    SMP, SMZ, SMY, SMYR, SMH, SMX,
    in_sem, out_sem, pair_send, pair_recv, halo_send, halo_recv, fwd_send, fwd_recv,
    w_send, w_recv, wo_send, wo_recv,
    z_send, z_recv, xy_send, xy_recv, zh_send, zh_recv, xg_send, xg_recv, go_send, go_recv,
    sm_send, sm_recv, op_send, op_recv,
):
    arrivals = []
    for i, (src, dst) in enumerate((
        (proj_in_hbm, proj_in), (proj_out_hbm, proj_out), (strands_hbm, strands),
        (cotangent_hbm, cotangent), (taps_hbm, taps_in), (filters_hbm, filters_in),
    )):
        copy = pltpu.make_async_copy(src, dst, in_sem.at[i])
        copy.start()
        arrivals.append(copy)
    departures = []

    def leave(i, src, dst):
        copy = pltpu.make_async_copy(src, dst, out_sem.at[i])
        copy.start()
        departures.append(copy)

    seq, ch = lax.axis_index("seq"), lax.axis_index("ch")
    z_hi, x = seq // 4, seq % 4
    z_lo, y, c = ch // 8, (ch // 2) % 4, ch % 2
    z = z_hi * 2 + z_lo
    b = z_lo * 4 + y
    chip = seq * 8 + b
    before, after = (chip + 127) % 128, (chip + 1) % 128
    partner = at_coords(x, y, z, 1 - c)
    z_above, z_below = (z + 1) % 8, (z + 7) % 8
    z_up, z_down = at_coords(x, y, z_above, c), at_coords(x, y, z_below, c)
    is_first = c == 0

    barrier = pltpu.get_barrier_semaphore()
    peers = [partner]
    for zz in (z_above, z_below):
        for cc in (0, 1):
            peers.append(at_coords(x, y, zz, cc))
    for dx in range(4):
        for dy in range(4):
            if dx or dy:
                peers.append(at_coords((x + dx) % 4, (y + dy) % 4, z, c))
    for d in range(1, 4):
        peers.append(at_coords(x, y, (z + 2 * d) % 8, c))
        peers.append(at_coords((x + d) % 4, y, z, 1 - c))
        peers.append(at_coords(x, (y + d) % 4, z, 1 - c))
    for q in (before, after):
        peers.append(at_chip(q, 0))
        peers.append(at_chip(q, 1))
    for peer in peers:
        pl.semaphore_signal(barrier, inc=1, device_id=peer, device_id_type=MESH)

    QM[...] = block_order()
    FLIP[...] = anti_identity(512)
    my_rows = pl.multiple_of(64 * b + 32 * c, 32)
    arrivals[0].wait()
    low, high = [], []
    for s in range(3):
        a, o = split_cores(proj_in[:, pl.ds(s * 1024, 1024)].astype(F32))
        low.append(a)
        high.append(o)
    moved = mm(jnp.concatenate(low + high, axis=0).astype(BF16), QM[...])
    for k in range(4):
        for s in range(3):
            lanes = pl.ds(128 * s, 128)
            even = moved[32 * s:32 * s + 32, 128 * k:128 * k + 128]
            odd = moved[96 + 32 * s:128 + 32 * s, 128 * k:128 * k + 128]
            W[k, pl.ds(my_rows, 32), lanes] = jnp.where(is_first, even, odd).astype(BF16)
            WSEND[k, :, lanes] = jnp.where(is_first, odd, even).astype(BF16)
    arrivals[1].wait()
    for k in range(4):
        WO[k, b] = proj_out[pl.ds(16 * k, 16), :]
    own = pl.multiple_of(144 + 128 * c, 16)
    own_c0 = pl.multiple_of(128 * c, 16)
    arrivals[2].wait()
    U[0, pl.ds(own, 128), :] = strands[0]
    U[1, pl.ds(own, 128), :] = mm(strands[1], FLIP[...]).astype(BF16)
    arrivals[3].wait()
    C[0, pl.ds(own_c0, 128), :] = cotangent[0]
    C[1, pl.ds(own, 128), :] = mm(cotangent[1], FLIP[...]).astype(BF16)
    arrivals[4].wait()
    arrivals[5].wait()
    pl.semaphore_wait(barrier, len(peers))

    def wo_half(m, bb, half):
        return WO.at[m, bb, :, pl.ds(256 * half, 256)]

    def w_half(m, bb, half):
        return W.at[m, pl.ds(pl.multiple_of(64 * bb + 32 * half, 32), 32), :]

    def gather_first(m):
        mine = W.at[m, pl.ds(my_rows, 32), :]
        theirs = WSEND.at[m]
        place = W.at[m, pl.ds(my_rows, 32), :]
        remote(theirs, place, w_send.at[m], w_recv.at[m, 0], partner)
        for d in (1, 3, 2):
            yy = (y + d) % 4
            remote(mine, place, w_send.at[m], w_recv.at[m, 0], at_coords(x, yy, z, c))
            remote(theirs, place, w_send.at[m], w_recv.at[m, 0], at_coords(x, yy, z, 1 - c))
            remote(WO.at[m, b], WO.at[m, b], wo_send.at[m], wo_recv.at[m, 0], at_coords(x, yy, z, c))
        z_side = jnp.where(is_first, z_above, z_below)
        remote(mine, place, w_send.at[m], w_recv.at[m, 1], at_coords(x, y, z_side, c))
        remote(theirs, place, w_send.at[m], w_recv.at[m, 1], at_coords(x, y, z_side, 1 - c))
        for half, side in ((0, z_up), (1, z_down)):
            remote(wo_half(m, b, half), wo_half(m, b, half), wo_send.at[m], wo_recv.at[m, 1], side)

    def gather_second(m):
        wait_bytes(W.at[m, pl.ds(0, 224), :], w_recv.at[m, 0])
        wait_bytes(WO.at[m, pl.ds(0, 3)], wo_recv.at[m, 0])
        for d in (1, 3, 2):
            bb = z_lo * 4 + (y + d) % 4
            for half, side in ((0, z_up), (1, z_down)):
                remote(w_half(m, bb, half), w_half(m, bb, half), w_send.at[m], w_recv.at[m, 1], side)
                remote(wo_half(m, bb, half), wo_half(m, bb, half), wo_send.at[m], wo_recv.at[m, 1], side)

    def gather_last(m):
        wait_bytes(W.at[m, pl.ds(0, 256), :], w_recv.at[m, 1])
        wait_bytes(WO.at[m, pl.ds(0, 4)], wo_recv.at[m, 1])

    def gather_sent(m):
        wait_bytes(W.at[m, pl.ds(0, 480), :], w_send.at[m])
        wait_bytes(WO.at[m, pl.ds(0, 7)], wo_send.at[m])

    gather_first(0)

    far = jnp.where(is_first, before, after)
    near = jnp.where(is_first, after, before)
    big_at = pl.multiple_of(jnp.where(is_first, 400, 16), 16)
    small_src = pl.multiple_of(own + jnp.where(is_first, 112, 0), 16)
    small_at = pl.multiple_of(jnp.where(is_first, 0, 528), 16)
    halo = []
    for s in range(2):
        halo.append(remote(
            U.at[s, pl.ds(own, 128), :], U.at[s, pl.ds(big_at, 128), :],
            halo_send.at[s], halo_recv.at[1 - c], at_chip(far, s)))
        halo.append(remote(
            U.at[s, pl.ds(small_src, 16), :], U.at[s, pl.ds(small_at, 16), :],
            halo_send.at[2 + s], halo_recv.at[2 + c], at_chip(near, s)))
    c_own = pl.multiple_of(jnp.where(is_first, 0, 272), 16)
    c_big = pl.multiple_of(jnp.where(is_first, 256, 16), 16)
    halo.append(remote(
        C.at[c, pl.ds(c_own, 128), :], C.at[c, pl.ds(c_big, 128), :],
        halo_send.at[4], halo_recv.at[4], at_chip(far, c)))
    c_small_src = pl.multiple_of(jnp.where(is_first, 144 + 112, 128), 16)
    c_small = pl.multiple_of(jnp.where(is_first, 0, 384), 16)
    halo.append(remote(
        C.at[1 - c, pl.ds(c_small_src, 16), :], C.at[1 - c, pl.ds(c_small, 16), :],
        halo_send.at[5], halo_recv.at[5], at_chip(near, 1 - c)))
    pair = [
        remote(U.at[s, pl.ds(own, 128), :], U.at[s, pl.ds(own, 128), :], pair_send.at[s], pair_recv.at[s], partner)
        for s in range(2)
    ]
    pair.append(remote(
        C.at[0, pl.ds(own_c0, 128), :], C.at[0, pl.ds(own_c0, 128), :], pair_send.at[2], pair_recv.at[2], partner))
    pair.append(remote(
        C.at[1, pl.ds(own, 128), :], C.at[1, pl.ds(own, 128), :], pair_send.at[3], pair_recv.at[3], partner))
    for m in range(1, 4):
        gather_first(m)

    picked = []
    for s in range(3):
        a, o = split_cores(taps_in[:, pl.ds(s * 1024, 1024)])
        picked.append(jnp.where(is_first, a, o))
    picked = exact_dot(jnp.concatenate(picked, axis=0), QM[...])
    for k in range(4):
        for s in range(3):
            TAPS[k, :, pl.ds(128 * s, 128)] = picked[4 * s:4 * s + 4, 128 * k:128 * k + 128]
    row = lax.broadcasted_iota(jnp.int32, (32, 64), 0)
    col = lax.broadcasted_iota(jnp.int32, (32, 64), 1)
    chosen = jnp.where((row % 8) * 8 + 4 * c + row // 8 == col, 1.0, 0.0).astype(BF16)
    build_tables(mm(chosen, filters_in[...]).astype(BF16), TF, TB)

    gather_second(0)
    wait_bytes(U.at[c, pl.ds(16, 128), :], halo_recv.at[0])
    wait_bytes(U.at[c, pl.ds(400, 128), :], halo_recv.at[1])
    wait_bytes(U.at[c, pl.ds(0, 16), :], halo_recv.at[2])
    wait_bytes(U.at[c, pl.ds(528, 16), :], halo_recv.at[3])
    wait_bytes(C.at[c, pl.ds(c_big, 128), :], halo_recv.at[4])
    wait_bytes(C.at[c, pl.ds(pl.multiple_of(jnp.where(is_first, 384, 0), 16), 16), :], halo_recv.at[5])
    c_halo = pl.multiple_of(jnp.where(is_first, 256, 0), 16)
    c_halo_other = pl.multiple_of(jnp.where(is_first, 0, 256), 16)
    fwd = []
    for i, at in enumerate((0, 400)):
        rows = U.at[c, pl.ds(at, 144), :]
        fwd.append(remote(rows, rows, fwd_send.at[i], fwd_recv.at[i], partner))
    rows = C.at[c, pl.ds(c_halo, 144), :]
    fwd.append(remote(rows, rows, fwd_send.at[2], fwd_recv.at[2], partner))
    for copy in pair:
        copy.wait_recv()
    for s in range(2):
        UT[:, pl.ds(256 * s, 256)] = jnp.transpose(U[s, pl.ds(144, 256), :])
    gather_second(1)
    for i, at in enumerate((0, 400)):
        wait_bytes(U.at[1 - c, pl.ds(at, 144), :], fwd_recv.at[i])
    wait_bytes(C.at[1 - c, pl.ds(c_halo_other, 144), :], fwd_recv.at[2])
    for copy in fwd:
        copy.wait_send()

    @pl.when(chip == 0)
    def _():
        U[:, pl.ds(0, 144), :] = jnp.zeros((2, 144, 512), BF16)
        C[1, pl.ds(0, 144), :] = jnp.zeros((144, 512), BF16)

    @pl.when(chip == 127)
    def _():
        U[:, pl.ds(400, 144), :] = jnp.zeros((2, 144, 512), BF16)
        C[0, pl.ds(256, 144), :] = jnp.zeros((144, 512), BF16)

    def z_start(k):
        SZ[k] = PART[k, pl.ds((1 - z_lo) * 4, 4)].astype(BF16)
        remote(SZ.at[k, :, pl.ds(0, 2)], RZ.at[k, :, pl.ds(0, 2)], z_send.at[k], z_recv.at[k, 0], z_up)
        remote(SZ.at[k, :, pl.ds(2, 2)], RZ.at[k, :, pl.ds(2, 2)], z_send.at[k], z_recv.at[k, 1], z_down)

    def xy_start(k):
        wait_bytes(RZ.at[k, :, pl.ds(0, 2)], z_recv.at[k, 0])
        wait_bytes(RZ.at[k, :, pl.ds(2, 2)], z_recv.at[k, 1])
        SXY[k] = (PART[k, pl.ds(z_lo * 4, 4)] + RZ[k].astype(F32)).astype(BF16)
        for dx in range(4):
            for dy in range(4):
                if dx or dy:
                    xx, yy = (x + dx) % 4, (y + dy) % 4
                    remote(SXY.at[k, yy, xx], RXY.at[k, 4 * dx + dy - 1],
                           xy_send.at[k], xy_recv.at[k], at_coords(xx, yy, z, c))

    def zh_start(k):
        wait_bytes(RXY.at[k], xy_recv.at[k])
        total = SXY[k, y, x].astype(F32)
        for i in range(15):
            total = total + RXY[k, i].astype(F32)
        ZH[k, z_hi] = total.astype(BF16)
        for d in range(1, 4):
            remote(ZH.at[k, z_hi], ZH.at[k, z_hi], zh_send.at[k], zh_recv.at[k], at_coords(x, y, (z + 2 * d) % 8, c))

    target = x // 2
    row_at = pl.multiple_of(16 * (x % 2), 16)
    go_at = pl.multiple_of(128 * x, 128)

    def xg_start(k):
        wait_bytes(ZH.at[k, pl.ds(0, 3)], zh_recv.at[k])
        total = ZH[k, 0].astype(F32)
        for i in range(1, 4):
            total = total + ZH[k, i].astype(F32)
        FS[k] = total.astype(BF16)
        part = FS.at[k, :, pl.ds(0, 384)]
        place = FIN.at[k, c, pl.ds(row_at, 16), :]
        piece = FS.at[k, :, pl.ds(384, 128)]
        spot = GO.at[k, :, pl.ds(go_at, 128)]
        for d in range(1, 4):
            remote(part, place, xg_send.at[k], xg_recv.at[k], at_coords((x + d) % 4, y, z, target))
            remote(piece, spot, go_send.at[k], go_recv.at[k], at_coords((x + d) % 4, y, z, c))

        @pl.when(c == target)
        def _():
            pltpu.make_async_copy(part, place, xg_recv.at[k]).start()

        @pl.when(c != target)
        def _():
            remote(part, place, xg_send.at[k], xg_recv.at[k], partner)

        GO[k, :, pl.ds(go_at, 128)] = FS[k, :, pl.ds(384, 128)]

    def reduced(k):
        wait_bytes(FIN.at[k], xg_recv.at[k])
        wait_bytes(GO.at[k, :, pl.ds(0, 384)], go_recv.at[k])

    def reduce_sent(k):
        wait_bytes(SZ.at[k], z_send.at[k])
        wait_bytes(RXY.at[k], xy_send.at[k])
        wait_bytes(ZH.at[k, pl.ds(0, 3)], zh_send.at[k])
        wait_bytes(FS.at[pl.ds(0, 3), :, pl.ds(0, 384)], xg_send.at[k])
        wait_bytes(FS.at[pl.ds(0, 3), :, pl.ds(384, 128)], go_send.at[k])

        @pl.when(c != target)
        def _():
            wait_bytes(FS.at[k, :, pl.ds(0, 384)], xg_send.at[k])

    def small_z():
        taps_rows = []
        for k in range(4):
            taps_rows.append(jnp.concatenate(
                [PSH[k, :, pl.ds(128 * s, 128)] for s in range(3)], axis=0))
        back = exact_dot(jnp.concatenate(taps_rows, axis=1), QM[...], NT)
        fil = [pltpu.roll(PFIL[k], 255, 1)[:, :128] for k in range(4)]
        for i in range(8):
            m = i // 2
            tiles = (3 * m, 3 * m + 1) if i % 2 == 0 else (3 * m + 1, 3 * m + 2)
            rows = []
            for t in tiles:
                s, p = t // 4, t % 4
                rows.append(back[4 * s:4 * s + 4, 128 * p:128 * p + 128])
            rows += [fil[k][i:i + 1] for k in range(4)]
            SMP[i] = jnp.concatenate(rows + [jnp.zeros((4, 128), F32)], axis=0)
        remote(SMP.at[pl.ds((1 - z_lo) * 4, 4)], SMZ, sm_send.at[0], sm_recv.at[0], z_up)

    def small_y():
        wait_bytes(SMZ, sm_recv.at[0])
        SMY[...] = SMP[pl.ds(z_lo * 4, 4)] + SMZ[...]
        for d in range(1, 4):
            yy = (y + d) % 4
            remote(SMY.at[yy], SMYR.at[d - 1], sm_send.at[1], sm_recv.at[1], at_coords(x, yy, z, c))

    def small_h():
        wait_bytes(SMYR, sm_recv.at[1])
        SMH[z_hi] = SMY[y] + SMYR[0] + SMYR[1] + SMYR[2]
        for d in range(1, 4):
            remote(SMH.at[z_hi], SMH.at[z_hi], sm_send.at[2], sm_recv.at[2], at_coords(x, y, (z + 2 * d) % 8, c))

    def small_x():
        wait_bytes(SMH.at[pl.ds(0, 3)], sm_recv.at[2])
        SMX[c, x] = SMH[0] + SMH[1] + SMH[2] + SMH[3]
        for d in range(1, 4):
            for cc in (c, 1 - c):
                remote(SMX.at[c, x], SMX.at[c, x], sm_send.at[3], sm_recv.at[3], at_coords((x + d) % 4, y, z, cc))
        remote(SMX.at[c, x], SMX.at[c, x], sm_send.at[3], sm_recv.at[3], partner)

    def small_last():
        wait_bytes(SMP.at[pl.ds(0, 7)], sm_recv.at[3])
        e = SMX[0, 0] + SMX[0, 1] + SMX[0, 2] + SMX[0, 3]
        o = SMX[1, 0] + SMX[1, 1] + SMX[1, 2] + SMX[1, 3]
        mine = jnp.where(is_first, e, o)
        gfil_ref[...] = exact_dot(mine, anti_identity(128))[8:12] * scale
        lane = lax.broadcasted_iota(jnp.int32, (4, 128), 1)

        def blocks(v):
            a, t = v[0:4], v[4:8]
            turned_a, turned_t = pltpu.roll(a, 64, 1), pltpu.roll(t, 64, 1)
            even = b % 2 == 0
            return (
                jnp.where(even, a, turned_a),
                jnp.where(even, turned_a, t),
                jnp.where(even, t, turned_t),
            )

        e, o = blocks(e), blocks(o)
        one = jnp.where(is_first, e[0], o[1])
        two = jnp.where(is_first, o[0], e[2])
        three = jnp.where(is_first, e[1], o[2])
        gshort_ref[:, pl.ds(0, 128)] = jnp.where(lane < 64, one, pltpu.roll(two, 64, 1)) * scale
        gshort_ref[:, pl.ds(128, 64)] = three[:, :64] * scale

    def small_sent():
        wait_bytes(SMZ, sm_send.at[0])
        wait_bytes(SMYR, sm_send.at[1])
        wait_bytes(SMYR, sm_send.at[2])
        wait_bytes(SMP.at[pl.ds(0, 7)], sm_send.at[3])


    def body(k, carry):
        gather_last(k)

        def hook_a():
            @pl.when(k == 0)
            def _():
                gather_second(2)

        def hook_b():
            @pl.when(k == 0)
            def _():
                gather_second(3)

        compute_chunk(k, U, C, W, WO, TAPS, TF, TB, UT, HID, GP, PART, PSH, PFIL, ROWS, hook_a, hook_b)
        z_start(k)

        @pl.when(k >= 2)
        def _():
            xy_start(k - 2)

        return carry

    lax.fori_loop(0, 4, body, 0)

    small_z()
    other_rows = 128 * (1 - c)
    op = []
    for o in range(2):
        if o == 0:
            res = mm(HID[0], WO[0].reshape(128, 512))
            for k in range(1, 4):
                res = res + mm(HID[k], WO[k].reshape(128, 512))
            xy_start(2)
        else:
            res = mm(GP[0], W[0], NT)
            for k in range(1, 4):
                res = res + mm(GP[k], W[k], NT)
        OUTP[o] = res
        for s in range(2):
            rows = pl.ds(pl.multiple_of(256 * s + other_rows, 128), 128)
            op.append(remote(OUTP.at[o, rows, :], RP.at[o, s], op_send.at[o, s], op_recv.at[o, s], partner))
    zh_start(0)
    xy_start(3)
    small_y()
    for o, (ref, hbm) in enumerate(((out_ref, out_hbm), (grad_ref, grad_hbm))):
        for s in range(2):
            op[2 * o + s].wait_recv()
            rows = pl.ds(pl.multiple_of(256 * s + 128 * c, 128), 128)
            value = (OUTP[o, rows, :] + RP[o, s]).astype(BF16)
            ref[s] = value if s == 0 else mm(value, FLIP[...]).astype(BF16)
        leave(o, ref, hbm)
    zh_start(1)
    xg_start(0)
    small_h()
    zh_start(2)
    xg_start(1)
    zh_start(3)
    small_x()
    xg_start(2)
    xg_start(3)
    for copy in pair + halo + op:
        copy.wait_send()
    for m in range(4):
        gather_sent(m)
    small_last()
    leave(4, gshort_ref, gshort_hbm)
    leave(5, gfil_ref, gfil_hbm)
    for k in range(4):
        reduced(k)
    for k in range(4):
        gout_ref[pl.ds(16 * k, 16), :] = GO[k].astype(F32) * scale
    leave(3, gout_ref, gout_hbm)
    rows = []
    for cc in range(2):
        for s in range(3):
            rows.append(jnp.concatenate([FIN[k, cc, :, pl.ds(128 * s, 128)] for k in range(4)], axis=1))
    back = mm(jnp.concatenate(rows, axis=0), QM[...], NT) * scale
    for s in range(3):
        for t in range(4):
            lanes = slice(128 * t, 128 * t + 128)
            first, second = halves(back[32 * s:32 * s + 32, lanes], back[96 + 32 * s:128 + 32 * s, lanes])
            gin_ref[:, pl.ds(s * 1024 + t * 256, 128)] = first
            gin_ref[:, pl.ds(s * 1024 + t * 256 + 128, 128)] = second
    leave(2, gin_ref, gin_hbm)
    for k in range(4):
        reduce_sent(k)
    small_sent()
    for copy in departures:
        copy.wait()


def hand_over(*refs):
    n = 6
    sources, targets, held = refs[:n], refs[n:2 * n], refs[2 * n:3 * n]
    in_sem, out_sem = refs[3 * n:]
    arrive = [pltpu.make_async_copy(sources[i], held[i], in_sem.at[i]) for i in range(n)]
    leave = [pltpu.make_async_copy(held[i], targets[i], out_sem.at[i]) for i in range(n)]
    for copy in arrive:
        copy.start()
    for i in range(n):
        arrive[i].wait()
        leave[i].start()
    for copy in leave:
        copy.wait()


def shards(strands, cotangent, proj_in, proj_out, short_taps, filters):
    length = strands.shape[1] * lax.axis_size(("seq", "ch"))
    scale = float(length) ** (-0.5)
    dma = pltpu.SemaphoreType.DMA
    outs = (
        jax.ShapeDtypeStruct((2, 128, 512), BF16),
        jax.ShapeDtypeStruct((2, 128, 512), BF16),
        jax.ShapeDtypeStruct((32, 3072), F32),
        jax.ShapeDtypeStruct((64, 512), F32),
        jax.ShapeDtypeStruct((4, 192), F32),
        jax.ShapeDtypeStruct((4, 128), F32),
    )
    scratch = [
        pltpu.VMEM((2, 128, 512), BF16),
        pltpu.VMEM((2, 128, 512), BF16),
        pltpu.VMEM((32, 3072), BF16),
        pltpu.VMEM((64, 512), BF16),
        pltpu.VMEM((4, 3072), F32),
        pltpu.VMEM((64, 128), BF16),
    ]
    scratch += [pltpu.VMEM(o.shape, o.dtype) for o in outs]
    scratch += [
        pltpu.VMEM((2, 544, 512), BF16),
        pltpu.VMEM((2, 400, 512), BF16),
        pltpu.VMEM((4, 512, 384), BF16),
        pltpu.VMEM((4, 8, 16, 512), BF16),
        pltpu.VMEM((4, 32, 384), BF16),
        pltpu.VMEM((512, 512), BF16),
        pltpu.VMEM((512, 512), BF16),
        pltpu.VMEM((4, 4, 384), F32),
        pltpu.VMEM((4, 1024, 256), BF16),
        pltpu.VMEM((4, 1024, 256), BF16),
        pltpu.VMEM((512, 512), BF16),
        pltpu.VMEM((4, 512, 128), BF16),
        pltpu.VMEM((4, 512, 384), BF16),
        pltpu.VMEM((4, 8, 4, 16, 512), F32),
        pltpu.VMEM((4, 4, 384), F32),
        pltpu.VMEM((4, 8, 256), F32),
        pltpu.VMEM((12, 432, 128), F32),
        pltpu.VMEM((2, 512, 512), F32),
        pltpu.VMEM((2, 2, 128, 512), F32),
        pltpu.VMEM((4, 4, 4, 16, 512), BF16),
        pltpu.VMEM((4, 4, 4, 16, 512), BF16),
        pltpu.VMEM((4, 4, 4, 16, 512), BF16),
        pltpu.VMEM((4, 15, 16, 512), BF16),
        pltpu.VMEM((4, 4, 16, 512), BF16),
        pltpu.VMEM((4, 16, 512), BF16),
        pltpu.VMEM((4, 2, 32, 384), BF16),
        pltpu.VMEM((4, 16, 512), BF16),
        pltpu.VMEM((8, 16, 128), F32),
        pltpu.VMEM((4, 16, 128), F32),
        pltpu.VMEM((4, 16, 128), F32),
        pltpu.VMEM((3, 16, 128), F32),
        pltpu.VMEM((4, 16, 128), F32),
        pltpu.VMEM((2, 4, 16, 128), F32),
    ]
    scratch += [
        dma((6,)), dma((6,)), dma((4,)), dma((4,)), dma((6,)), dma((6,)), dma((3,)), dma((3,)),
        dma((4,)), dma((4, 2)), dma((4,)), dma((4, 2)),
        dma((4,)), dma((4, 2)), dma((4,)), dma((4,)), dma((4,)), dma((4,)), dma((4,)), dma((4,)), dma((4,)), dma((4,)),
        dma((4,)), dma((4,)), dma((2, 2)), dma((2, 2)),
    ]
    anywhere = pl.BlockSpec(memory_space=pl.ANY)
    results = pl.pallas_call(
        functools.partial(kernel, scale),
        out_shape=outs,
        in_specs=[anywhere] * 6,
        out_specs=tuple([anywhere] * 6),
        scratch_shapes=scratch,
        compiler_params=pltpu.CompilerParams(
            collective_id=0, has_side_effects=True, vmem_limit_bytes=58 * 2**20
        ),
        cost_estimate=pl.CostEstimate(flops=9 * 10**9, bytes_accessed=4 * 10**6, transcendentals=0),
    )(strands, cotangent, proj_in, proj_out, short_taps.T, filters)
    results = pl.pallas_call(
        hand_over,
        out_shape=outs,
        in_specs=[anywhere] * 6,
        out_specs=tuple([anywhere] * 6),
        scratch_shapes=[pltpu.VMEM(o.shape, o.dtype) for o in outs] + [dma((6,)), dma((6,))],
    )(*results)
    return results[:4] + (results[4].T, results[5])


def solution(mesh):
    placed = P(None, ("seq", "ch"), None)
    rows = P("ch", None)
    return jax.shard_map(
        shards,
        mesh=mesh,
        in_specs=(placed, placed, rows, rows, P(), P()),
        out_specs=(placed, placed, rows, rows, rows, rows),
        check_vma=False,
    )
```

```python
import functools

import jax
import jax.numpy as jnp
from jax import lax
from jax.experimental import pallas as pl
from jax.experimental.pallas import tpu as pltpu
from jax.sharding import PartitionSpec as P

F32 = jnp.float32
BF16 = jnp.bfloat16
NN = (((1,), (0,)), ((), ()))
NT = (((1,), (1,)), ((), ()))
TN = (((0,), (0,)), ((), ()))


def mm(a, b, dims=NN):
    return lax.dot_general(a, b, dims, preferred_element_type=F32)


def lane_group(shape, span):
    return (lax.broadcasted_iota(jnp.int32, shape, 1) % span) // 16


def halves(tile, other):
    lane = lax.broadcasted_iota(jnp.int32, tile.shape, 1)
    low = jnp.where(lane < 64, tile, pltpu.roll(other, 64, 1))
    high = jnp.where(lane < 64, pltpu.roll(tile, 64, 1), other)
    return low, high


def build_tables(filters, TF, TB):
    t = lax.broadcasted_iota(jnp.int32, (128, 256), 0)
    k = lax.broadcasted_iota(jnp.int32, (128, 256), 1)
    to_f = jnp.where(t + k == 128, 1.0, 0.0).astype(BF16)
    to_b = jnp.where(t == k, 1.0, 0.0).astype(BF16)
    pat_f = mm(filters, to_f)
    pat_b = mm(filters, to_b)
    for g in range(32):
        for pat, table in ((pat_f, TF), (pat_b, TB)):
            rows = jnp.broadcast_to(pat[g:g + 1], (128, 256))
            skewed = pltpu.roll(rows, 0, 1, stride=1, stride_axis=0)
            table[g // 8, pl.ds((g % 8) * 128, 128), :] = skewed.astype(BF16)


def anti_identity(n):
    r = lax.broadcasted_iota(jnp.int32, (n, n), 0)
    c = lax.broadcasted_iota(jnp.int32, (n, n), 1)
    return jnp.where(r + c == n - 1, 1.0, 0.0).astype(BF16)


def diag(products, rows, count):
    group = lane_group((rows, products.shape[1]), 16 * count)
    out = products[0:rows]
    for g in range(1, count):
        out = jnp.where(group == g, products[g * rows:(g + 1) * rows], out)
    return out


def compute_chunk(k, U, C, Win, Wout, taps_ref, TF, TB, UT, HID, GP, PART, PSH, PFIL, ROWS, hook_a, hook_b):
    w = Win[k]
    wo = Wout[k].reshape(128, 512)
    taps = taps_ref[k]
    tf = TF[k]
    tb = TB[k]
    own_proj, gated, gc, keys, values, queries, ghs = [], [], [], [], [], [], []
    for s in range(2):
        sign = 1 if s == 0 else -1
        kv_at = 0 if s == 0 else 128
        q_at = 128 - kv_at
        pkv = mm(U[s, pl.ds(kv_at, 416), :], w[:, 128:]).astype(BF16)
        pq = mm(U[s, pl.ds(q_at, 416), :], w[:, :128]).astype(BF16)
        gh = mm(C[s], wo, NT).astype(BF16).astype(F32)
        mixed = []
        own_kv = 144 if s == 0 else 16
        own_q = 160 - own_kv
        for part, values_in in enumerate((pq, pkv[:, :128], pkv[:, 128:])):
            held = ROWS.at[3 * s + part]
            wide = values_in.astype(F32)
            held[pl.ds(8, 416), :] = wide
            t = taps[:, 128 * part:128 * part + 128]
            total = t[0:1] * wide
            for j in range(1, 4):
                total = total + t[j:j + 1] * held[pl.ds(8 - sign * j, 416), :]
            mixed.append(total)
        mq, key, value = mixed
        own_proj.append((own_q, own_kv, own_kv))
        gated.append((key * value).astype(BF16))
        keys.append(key)
        values.append(value)
        queries.append(mq)
        ghs.append(gh)
        at = 16 if s == 0 else 0
        gc.append((gh * mq[at:at + 400]).astype(BF16))
    hook_a()
    def packed(first, second):
        low_first, high_first = halves(*first)
        low_second, high_second = halves(*second)
        return (
            jnp.concatenate([low_first, low_second], axis=1),
            jnp.concatenate([high_first, high_second], axis=1),
        )

    def blocks_of(value, at, rows):
        return value[at:at + rows], value[at + 128:at + 128 + rows]

    xf = packed(blocks_of(gated[0], 16, 256), blocks_of(gc[1], 16, 256))
    xb = packed(blocks_of(gc[0], 0, 256), blocks_of(gated[1], 16, 256))
    left = packed(blocks_of(gc[0], 0, 128), blocks_of(gated[1], 16, 128))
    reverse = anti_identity(128)
    group = lane_group((128, 256), 64)
    yf, yb, prods = [], [], []
    for h in range(2):
        yf.append(diag(mm(tf[512 * h:512 * h + 512], xf[h]), 128, 4))
        yb.append(diag(mm(tb[512 * h:512 * h + 512], xb[h]), 128, 4))
        turned = mm(reverse, left[h]).astype(BF16)
        masked = jnp.concatenate([jnp.where(group == g, turned, jnp.zeros_like(turned)) for g in range(4)], axis=0)
        prods.append(mm(masked, xf[h], NT))
    f_first_strand = halves(yf[0][:, :128], yf[1][:, :128])
    f_second_strand = halves(yf[0][:, 128:], yf[1][:, 128:])
    b_first_strand = halves(yb[0][:, :128], yb[1][:, :128])
    b_second_strand = halves(yb[0][:, 128:], yb[1][:, 128:])
    tf3 = tf.reshape(8, 128, 256)
    tb3 = tb.reshape(8, 128, 256)
    f_last = tf3[:, 112:].reshape(128, 256)
    f_first = tf3[:, :16].reshape(128, 256)
    b_last = tb3[:, 112:].reshape(128, 256)
    b_first = tb3[:, :16].reshape(128, 256)
    conv0_x = diag(mm(f_last, gated[0][160:416]), 16, 8)
    gg1_x = diag(mm(f_first, gc[1][0:256]), 16, 8)
    gg0_x = diag(mm(b_last, gc[0][144:400]), 16, 8)
    conv1_x = diag(mm(b_first, gated[1][0:256]), 16, 8)
    conv = [
        jnp.concatenate([*f_first_strand, conv0_x], axis=0),
        jnp.concatenate([conv1_x, *b_second_strand], axis=0),
    ]
    gg = [
        jnp.concatenate([*b_first_strand, gg0_x], axis=0),
        jnp.concatenate([gg1_x, *f_second_strand], axis=0),
    ]
    hook_b()
    short = [[None] * 3 for _ in range(4)]
    for s in range(2):
        sign = 1 if s == 0 else -1
        own = 0 if s == 0 else 16
        q_at = 16 if s == 0 else 128
        kv_at = 144 if s == 0 else 0
        gh_at = 0 if s == 0 else 128
        query = queries[s][q_at:q_at + 272]
        hidden = (query[own:own + 256] * conv[s][own:own + 256]).astype(BF16)
        HID[k, pl.ds(256 * s, 256), :] = hidden
        grads = (
            ghs[s][gh_at:gh_at + 272] * conv[s],
            gg[s] * values[s][kv_at:kv_at + 272],
            gg[s] * keys[s][kv_at:kv_at + 272],
        )
        for part in range(3):
            held = ROWS.at[6 + 3 * s + part]
            p_own = ROWS[3 * s + part, pl.ds(8 + own_proj[s][part], 256), :]
            gm = grads[part].astype(BF16).astype(F32)
            held[pl.ds(8, 272), :] = gm
            t = taps[:, 128 * part:128 * part + 128]
            total = None
            for j in range(4):
                moved = gm[own:own + 256] if j == 0 else held[pl.ds(8 + own + sign * j, 256), :]
                term = t[j:j + 1] * moved
                total = term if total is None else total + term
                column = jnp.sum(p_own * moved, axis=0, keepdims=True)
                short[j][part] = column if s == 0 else short[j][part] + column
            GP[k, pl.ds(256 * s, 256), pl.ds(128 * part, 128)] = total.astype(BF16)
    for j in range(4):
        for part in range(3):
            PSH[k, pl.ds(j, 1), pl.ds(128 * part, 128)] = short[j][part]
    PART[k, :, :, :, pl.ds(0, 384)] = mm(UT[...], GP[k]).reshape(8, 4, 16, 384)
    po = mm(HID[k, pl.ds(0, 256), :], C[0, pl.ds(0, 256), :], TN)
    po = po + mm(HID[k, pl.ds(256, 256), :], C[1, pl.ds(144, 256), :], TN)
    for q in range(4):
        PART[k, :, q, :, pl.ds(384, 128)] = po[:, 128 * q:128 * q + 128].reshape(8, 16, 128)
    rows = []
    for g in range(8):
        r = pltpu.roll(prods[g // 4][128 * (g % 4):128 * (g % 4) + 128], 129, 1, stride=1, stride_axis=0)
        rows.append(jnp.sum(r, axis=0, keepdims=True))
    PFIL[k] = jnp.concatenate(rows, axis=0)


MESH = pl.DeviceIdType.MESH


def remote(src, dst, send, recv, device):
    copy = pltpu.make_async_remote_copy(
        src_ref=src, dst_ref=dst, send_sem=send, recv_sem=recv, device_id=device, device_id_type=MESH
    )
    copy.start()
    return copy


def wait_bytes(ref, sem):
    pltpu.make_async_copy(ref, ref, sem).wait()


def at_coords(x, y, z, c):
    return ((z // 2) * 4 + x, (z % 2) * 8 + y * 2 + c)


def at_chip(p, c):
    return (p // 8, (p % 8) * 2 + c)


def split_cores(wide):
    low, high = [], []
    for t in range(4):
        a, b = halves(wide[:, 256 * t:256 * t + 128], wide[:, 256 * t + 128:256 * t + 256])
        low.append(a)
        high.append(b)
    return jnp.concatenate(low, axis=1), jnp.concatenate(high, axis=1)


def exact_dot(value, zero_one, dims=NN):
    first = value.astype(BF16)
    rest = value - first.astype(F32)
    second = rest.astype(BF16)
    third = (rest - second.astype(F32)).astype(BF16)
    return mm(first, zero_one, dims) + mm(second, zero_one, dims) + mm(third, zero_one, dims)


def block_order():
    row = lax.broadcasted_iota(jnp.int32, (512, 512), 0)
    col = lax.broadcasted_iota(jnp.int32, (512, 512), 1)
    goes = ((row // 16) % 4) * 128 + (row // 64) * 16 + row % 16
    return jnp.where(goes == col, 1.0, 0.0).astype(BF16)


def kernel(
    scale,
    strands_hbm, cotangent_hbm, proj_in_hbm, proj_out_hbm, taps_hbm, filters_hbm,
    out_ref, grad_ref, gin_ref, gout_ref, gshort_ref, gfil_ref,
    strands, cotangent, proj_in, proj_out, taps_in, filters_in,
    U, C, W, WO, WSEND, QM, FLIP, TAPS, TF, TB, UT, HID, GP, PART, PSH, PFIL, ROWS, OUTP, RP,
    SZ, RZ, SXY, RXY, ZH, FS, FIN, GO,
    SMP, SMZ, SMY, SMYR, SMH, SMX,
    in_sem, pair_send, pair_recv, halo_send, halo_recv, fwd_send, fwd_recv,
    w_send, w_recv, wo_send, wo_recv,
    z_send, z_recv, xy_send, xy_recv, zh_send, zh_recv, xg_send, xg_recv, go_send, go_recv,
    sm_send, sm_recv, op_send, op_recv,
):
    arrivals = []
    for i, (src, dst) in enumerate((
        (proj_in_hbm, proj_in), (proj_out_hbm, proj_out), (strands_hbm, strands),
        (cotangent_hbm, cotangent), (taps_hbm, taps_in), (filters_hbm, filters_in),
    )):
        copy = pltpu.make_async_copy(src, dst, in_sem.at[i])
        copy.start()
        arrivals.append(copy)
    seq, ch = lax.axis_index("seq"), lax.axis_index("ch")
    z_hi, x = seq // 4, seq % 4
    z_lo, y, c = ch // 8, (ch // 2) % 4, ch % 2
    z = z_hi * 2 + z_lo
    b = z_lo * 4 + y
    chip = seq * 8 + b
    before, after = (chip + 127) % 128, (chip + 1) % 128
    partner = at_coords(x, y, z, 1 - c)
    z_above, z_below = (z + 1) % 8, (z + 7) % 8
    z_up, z_down = at_coords(x, y, z_above, c), at_coords(x, y, z_below, c)
    is_first = c == 0

    barrier = pltpu.get_barrier_semaphore()
    peers = [partner]
    for zz in (z_above, z_below):
        for cc in (0, 1):
            peers.append(at_coords(x, y, zz, cc))
    for dx in range(4):
        for dy in range(4):
            if dx or dy:
                peers.append(at_coords((x + dx) % 4, (y + dy) % 4, z, c))
    for d in range(1, 4):
        peers.append(at_coords(x, y, (z + 2 * d) % 8, c))
        peers.append(at_coords((x + d) % 4, y, z, 1 - c))
        peers.append(at_coords(x, (y + d) % 4, z, 1 - c))
    for q in (before, after):
        peers.append(at_chip(q, 0))
        peers.append(at_chip(q, 1))
    for peer in peers:
        pl.semaphore_signal(barrier, inc=1, device_id=peer, device_id_type=MESH)

    QM[...] = block_order()
    FLIP[...] = anti_identity(512)
    my_rows = pl.multiple_of(64 * b + 32 * c, 32)
    arrivals[0].wait()
    low, high = [], []
    for s in range(3):
        a, o = split_cores(proj_in[:, pl.ds(s * 1024, 1024)].astype(F32))
        low.append(a)
        high.append(o)
    moved = mm(jnp.concatenate(low + high, axis=0).astype(BF16), QM[...])
    for k in range(4):
        for s in range(3):
            lanes = pl.ds(128 * s, 128)
            even = moved[32 * s:32 * s + 32, 128 * k:128 * k + 128]
            odd = moved[96 + 32 * s:128 + 32 * s, 128 * k:128 * k + 128]
            W[k, pl.ds(my_rows, 32), lanes] = jnp.where(is_first, even, odd).astype(BF16)
            WSEND[k, :, lanes] = jnp.where(is_first, odd, even).astype(BF16)
    arrivals[1].wait()
    for k in range(4):
        WO[k, b] = proj_out[pl.ds(16 * k, 16), :]
    own = pl.multiple_of(144 + 128 * c, 16)
    own_c0 = pl.multiple_of(128 * c, 16)
    arrivals[2].wait()
    U[0, pl.ds(own, 128), :] = strands[0]
    U[1, pl.ds(own, 128), :] = mm(strands[1], FLIP[...]).astype(BF16)
    arrivals[3].wait()
    C[0, pl.ds(own_c0, 128), :] = cotangent[0]
    C[1, pl.ds(own, 128), :] = mm(cotangent[1], FLIP[...]).astype(BF16)
    arrivals[4].wait()
    arrivals[5].wait()
    pl.semaphore_wait(barrier, len(peers))

    def wo_half(m, bb, half):
        return WO.at[m, bb, :, pl.ds(256 * half, 256)]

    def w_half(m, bb, half):
        return W.at[m, pl.ds(pl.multiple_of(64 * bb + 32 * half, 32), 32), :]

    def gather_first(m):
        mine = W.at[m, pl.ds(my_rows, 32), :]
        theirs = WSEND.at[m]
        place = W.at[m, pl.ds(my_rows, 32), :]
        remote(theirs, place, w_send.at[m], w_recv.at[m, 0], partner)
        for d in (1, 3, 2):
            yy = (y + d) % 4
            kind = 2 if d == 2 else 0
            remote(mine, place, w_send.at[m], w_recv.at[m, kind], at_coords(x, yy, z, c))
            remote(theirs, place, w_send.at[m], w_recv.at[m, kind], at_coords(x, yy, z, 1 - c))
            remote(WO.at[m, b], WO.at[m, b], wo_send.at[m], wo_recv.at[m, kind], at_coords(x, yy, z, c))
        z_side = jnp.where(is_first, z_above, z_below)
        remote(mine, place, w_send.at[m], w_recv.at[m, 1], at_coords(x, y, z_side, c))
        remote(theirs, place, w_send.at[m], w_recv.at[m, 1], at_coords(x, y, z_side, 1 - c))
        for half, side in ((0, z_up), (1, z_down)):
            remote(wo_half(m, b, half), wo_half(m, b, half), wo_send.at[m], wo_recv.at[m, 1], side)

    def gather_second(m):
        wait_bytes(W.at[m, pl.ds(0, 160), :], w_recv.at[m, 0])
        wait_bytes(WO.at[m, pl.ds(0, 2)], wo_recv.at[m, 0])
        for d in (1, 3, 2):
            if d == 2:
                wait_bytes(W.at[m, pl.ds(0, 64), :], w_recv.at[m, 2])
                wait_bytes(WO.at[m, 0], wo_recv.at[m, 2])
            bb = z_lo * 4 + (y + d) % 4
            for half, side in ((0, z_up), (1, z_down)):
                remote(w_half(m, bb, half), w_half(m, bb, half), w_send.at[m], w_recv.at[m, 1], side)
                remote(wo_half(m, bb, half), wo_half(m, bb, half), wo_send.at[m], wo_recv.at[m, 1], side)

    def gather_last(m):
        wait_bytes(W.at[m, pl.ds(0, 256), :], w_recv.at[m, 1])
        wait_bytes(WO.at[m, pl.ds(0, 4)], wo_recv.at[m, 1])

    def gather_sent(m):
        wait_bytes(W.at[m, pl.ds(0, 480), :], w_send.at[m])
        wait_bytes(WO.at[m, pl.ds(0, 7)], wo_send.at[m])

    gather_first(0)

    far = jnp.where(is_first, before, after)
    near = jnp.where(is_first, after, before)
    big_at = pl.multiple_of(jnp.where(is_first, 400, 16), 16)
    small_src = pl.multiple_of(own + jnp.where(is_first, 112, 0), 16)
    small_at = pl.multiple_of(jnp.where(is_first, 0, 528), 16)
    halo = []
    for s in range(2):
        halo.append(remote(
            U.at[s, pl.ds(own, 128), :], U.at[s, pl.ds(big_at, 128), :],
            halo_send.at[s], halo_recv.at[1 - c], at_chip(far, s)))
        halo.append(remote(
            U.at[s, pl.ds(small_src, 16), :], U.at[s, pl.ds(small_at, 16), :],
            halo_send.at[2 + s], halo_recv.at[2 + c], at_chip(near, s)))
    c_own = pl.multiple_of(jnp.where(is_first, 0, 272), 16)
    c_big = pl.multiple_of(jnp.where(is_first, 256, 16), 16)
    halo.append(remote(
        C.at[c, pl.ds(c_own, 128), :], C.at[c, pl.ds(c_big, 128), :],
        halo_send.at[4], halo_recv.at[4], at_chip(far, c)))
    c_small_src = pl.multiple_of(jnp.where(is_first, 144 + 112, 128), 16)
    c_small = pl.multiple_of(jnp.where(is_first, 0, 384), 16)
    halo.append(remote(
        C.at[1 - c, pl.ds(c_small_src, 16), :], C.at[1 - c, pl.ds(c_small, 16), :],
        halo_send.at[5], halo_recv.at[5], at_chip(near, 1 - c)))
    pair = [
        remote(U.at[s, pl.ds(own, 128), :], U.at[s, pl.ds(own, 128), :], pair_send.at[s], pair_recv.at[s], partner)
        for s in range(2)
    ]
    pair.append(remote(
        C.at[0, pl.ds(own_c0, 128), :], C.at[0, pl.ds(own_c0, 128), :], pair_send.at[2], pair_recv.at[2], partner))
    pair.append(remote(
        C.at[1, pl.ds(own, 128), :], C.at[1, pl.ds(own, 128), :], pair_send.at[3], pair_recv.at[3], partner))
    for m in range(1, 4):
        gather_first(m)

    picked = []
    for s in range(3):
        a, o = split_cores(taps_in[:, pl.ds(s * 1024, 1024)])
        picked.append(jnp.where(is_first, a, o))
    picked = exact_dot(jnp.concatenate(picked, axis=0), QM[...])
    for k in range(4):
        for s in range(3):
            TAPS[k, :, pl.ds(128 * s, 128)] = picked[4 * s:4 * s + 4, 128 * k:128 * k + 128]
    row = lax.broadcasted_iota(jnp.int32, (32, 64), 0)
    col = lax.broadcasted_iota(jnp.int32, (32, 64), 1)
    chosen = jnp.where((row % 8) * 8 + 4 * c + row // 8 == col, 1.0, 0.0).astype(BF16)
    build_tables(mm(chosen, filters_in[...]).astype(BF16), TF, TB)

    gather_second(0)
    wait_bytes(U.at[c, pl.ds(16, 128), :], halo_recv.at[0])
    wait_bytes(U.at[c, pl.ds(400, 128), :], halo_recv.at[1])
    wait_bytes(U.at[c, pl.ds(0, 16), :], halo_recv.at[2])
    wait_bytes(U.at[c, pl.ds(528, 16), :], halo_recv.at[3])
    wait_bytes(C.at[c, pl.ds(c_big, 128), :], halo_recv.at[4])
    wait_bytes(C.at[c, pl.ds(pl.multiple_of(jnp.where(is_first, 384, 0), 16), 16), :], halo_recv.at[5])
    c_halo = pl.multiple_of(jnp.where(is_first, 256, 0), 16)
    c_halo_other = pl.multiple_of(jnp.where(is_first, 0, 256), 16)
    fwd = []
    for i, at in enumerate((0, 400)):
        rows = U.at[c, pl.ds(at, 144), :]
        fwd.append(remote(rows, rows, fwd_send.at[i], fwd_recv.at[i], partner))
    rows = C.at[c, pl.ds(c_halo, 144), :]
    fwd.append(remote(rows, rows, fwd_send.at[2], fwd_recv.at[2], partner))
    for copy in pair:
        copy.wait_recv()
    for s in range(2):
        UT[:, pl.ds(256 * s, 256)] = jnp.transpose(U[s, pl.ds(144, 256), :])
    gather_second(1)
    for i, at in enumerate((0, 400)):
        wait_bytes(U.at[1 - c, pl.ds(at, 144), :], fwd_recv.at[i])
    wait_bytes(C.at[1 - c, pl.ds(c_halo_other, 144), :], fwd_recv.at[2])
    for copy in fwd:
        copy.wait_send()

    @pl.when(chip == 0)
    def _():
        U[:, pl.ds(0, 144), :] = jnp.zeros((2, 144, 512), BF16)
        C[1, pl.ds(0, 144), :] = jnp.zeros((144, 512), BF16)

    @pl.when(chip == 127)
    def _():
        U[:, pl.ds(400, 144), :] = jnp.zeros((2, 144, 512), BF16)
        C[0, pl.ds(256, 144), :] = jnp.zeros((144, 512), BF16)

    def z_start(k):
        SZ[k] = PART[k, pl.ds((1 - z_lo) * 4, 4)].astype(BF16)
        remote(SZ.at[k, :, pl.ds(0, 2)], RZ.at[k, :, pl.ds(0, 2)], z_send.at[k], z_recv.at[k, 0], z_up)
        remote(SZ.at[k, :, pl.ds(2, 2)], RZ.at[k, :, pl.ds(2, 2)], z_send.at[k], z_recv.at[k, 1], z_down)

    def xy_start(k):
        wait_bytes(RZ.at[k, :, pl.ds(0, 2)], z_recv.at[k, 0])
        wait_bytes(RZ.at[k, :, pl.ds(2, 2)], z_recv.at[k, 1])
        SXY[k] = (PART[k, pl.ds(z_lo * 4, 4)] + RZ[k].astype(F32)).astype(BF16)
        for dx in range(4):
            for dy in range(4):
                if dx or dy:
                    xx, yy = (x + dx) % 4, (y + dy) % 4
                    remote(SXY.at[k, yy, xx], RXY.at[k, 4 * dx + dy - 1],
                           xy_send.at[k], xy_recv.at[k], at_coords(xx, yy, z, c))

    def zh_start(k):
        wait_bytes(RXY.at[k], xy_recv.at[k])
        total = SXY[k, y, x].astype(F32)
        for i in range(15):
            total = total + RXY[k, i].astype(F32)
        ZH[k, z_hi] = total.astype(BF16)
        for d in range(1, 4):
            remote(ZH.at[k, z_hi], ZH.at[k, z_hi], zh_send.at[k], zh_recv.at[k], at_coords(x, y, (z + 2 * d) % 8, c))

    target = x // 2
    row_at = pl.multiple_of(16 * (x % 2), 16)
    go_at = pl.multiple_of(128 * x, 128)

    def xg_start(k):
        wait_bytes(ZH.at[k, pl.ds(0, 3)], zh_recv.at[k])
        total = ZH[k, 0].astype(F32)
        for i in range(1, 4):
            total = total + ZH[k, i].astype(F32)
        FS[k] = total.astype(BF16)
        part = FS.at[k, :, pl.ds(0, 384)]
        place = FIN.at[k, c, pl.ds(row_at, 16), :]
        piece = FS.at[k, :, pl.ds(384, 128)]
        spot = GO.at[k, :, pl.ds(go_at, 128)]
        for d in range(1, 4):
            remote(part, place, xg_send.at[k], xg_recv.at[k], at_coords((x + d) % 4, y, z, target))
            remote(piece, spot, go_send.at[k], go_recv.at[k], at_coords((x + d) % 4, y, z, c))

        @pl.when(c == target)
        def _():
            pltpu.make_async_copy(part, place, xg_recv.at[k]).start()

        @pl.when(c != target)
        def _():
            remote(part, place, xg_send.at[k], xg_recv.at[k], partner)

        GO[k, :, pl.ds(go_at, 128)] = FS[k, :, pl.ds(384, 128)]

    def reduced(k):
        wait_bytes(FIN.at[k], xg_recv.at[k])
        wait_bytes(GO.at[k, :, pl.ds(0, 384)], go_recv.at[k])

    def reduce_sent(k):
        wait_bytes(SZ.at[k], z_send.at[k])
        wait_bytes(RXY.at[k], xy_send.at[k])
        wait_bytes(ZH.at[k, pl.ds(0, 3)], zh_send.at[k])
        wait_bytes(FS.at[pl.ds(0, 3), :, pl.ds(0, 384)], xg_send.at[k])
        wait_bytes(FS.at[pl.ds(0, 3), :, pl.ds(384, 128)], go_send.at[k])

        @pl.when(c != target)
        def _():
            wait_bytes(FS.at[k, :, pl.ds(0, 384)], xg_send.at[k])

    def small_z():
        taps_rows = []
        for k in range(4):
            taps_rows.append(jnp.concatenate(
                [PSH[k, :, pl.ds(128 * s, 128)] for s in range(3)], axis=0))
        back = exact_dot(jnp.concatenate(taps_rows, axis=1), QM[...], NT)
        fil = [pltpu.roll(PFIL[k], 255, 1)[:, :128] for k in range(4)]
        for i in range(8):
            m = i // 2
            tiles = (3 * m, 3 * m + 1) if i % 2 == 0 else (3 * m + 1, 3 * m + 2)
            rows = []
            for t in tiles:
                s, p = t // 4, t % 4
                rows.append(back[4 * s:4 * s + 4, 128 * p:128 * p + 128])
            rows += [fil[k][i:i + 1] for k in range(4)]
            SMP[i] = jnp.concatenate(rows + [jnp.zeros((4, 128), F32)], axis=0)
        remote(SMP.at[pl.ds((1 - z_lo) * 4, 4)], SMZ, sm_send.at[0], sm_recv.at[0], z_up)

    def small_y():
        wait_bytes(SMZ, sm_recv.at[0])
        SMY[...] = SMP[pl.ds(z_lo * 4, 4)] + SMZ[...]
        for d in range(1, 4):
            yy = (y + d) % 4
            remote(SMY.at[yy], SMYR.at[d - 1], sm_send.at[1], sm_recv.at[1], at_coords(x, yy, z, c))

    def small_h():
        wait_bytes(SMYR, sm_recv.at[1])
        SMH[z_hi] = SMY[y] + SMYR[0] + SMYR[1] + SMYR[2]
        for d in range(1, 4):
            remote(SMH.at[z_hi], SMH.at[z_hi], sm_send.at[2], sm_recv.at[2], at_coords(x, y, (z + 2 * d) % 8, c))

    def small_x():
        wait_bytes(SMH.at[pl.ds(0, 3)], sm_recv.at[2])
        SMX[c, x] = SMH[0] + SMH[1] + SMH[2] + SMH[3]
        for d in range(1, 4):
            for cc in (c, 1 - c):
                remote(SMX.at[c, x], SMX.at[c, x], sm_send.at[3], sm_recv.at[3], at_coords((x + d) % 4, y, z, cc))
        remote(SMX.at[c, x], SMX.at[c, x], sm_send.at[3], sm_recv.at[3], partner)

    def small_last():
        wait_bytes(SMP.at[pl.ds(0, 7)], sm_recv.at[3])
        e = SMX[0, 0] + SMX[0, 1] + SMX[0, 2] + SMX[0, 3]
        o = SMX[1, 0] + SMX[1, 1] + SMX[1, 2] + SMX[1, 3]
        mine = jnp.where(is_first, e, o)
        gfil_ref[...] = exact_dot(mine, anti_identity(128))[8:12] * scale
        lane = lax.broadcasted_iota(jnp.int32, (4, 128), 1)

        def blocks(v):
            a, t = v[0:4], v[4:8]
            turned_a, turned_t = pltpu.roll(a, 64, 1), pltpu.roll(t, 64, 1)
            even = b % 2 == 0
            return (
                jnp.where(even, a, turned_a),
                jnp.where(even, turned_a, t),
                jnp.where(even, t, turned_t),
            )

        e, o = blocks(e), blocks(o)
        one = jnp.where(is_first, e[0], o[1])
        two = jnp.where(is_first, o[0], e[2])
        three = jnp.where(is_first, e[1], o[2])
        gshort_ref[:, pl.ds(0, 128)] = jnp.where(lane < 64, one, pltpu.roll(two, 64, 1)) * scale
        gshort_ref[:, pl.ds(128, 64)] = three[:, :64] * scale

    def small_sent():
        wait_bytes(SMZ, sm_send.at[0])
        wait_bytes(SMYR, sm_send.at[1])
        wait_bytes(SMYR, sm_send.at[2])
        wait_bytes(SMP.at[pl.ds(0, 7)], sm_send.at[3])


    def body(k, carry):
        gather_last(k)

        def hook_a():
            @pl.when(k == 0)
            def _():
                gather_second(2)

            @pl.when(k == 1)
            def _():
                gather_second(3)

        def hook_b():
            pass

        compute_chunk(k, U, C, W, WO, TAPS, TF, TB, UT, HID, GP, PART, PSH, PFIL, ROWS, hook_a, hook_b)
        z_start(k)

        @pl.when(k >= 2)
        def _():
            xy_start(k - 2)

        return carry

    lax.fori_loop(0, 4, body, 0)

    small_z()
    other_rows = 128 * (1 - c)
    op = []
    for o in range(2):
        if o == 0:
            res = mm(HID[0], WO[0].reshape(128, 512))
            for k in range(1, 4):
                res = res + mm(HID[k], WO[k].reshape(128, 512))
            xy_start(2)
        else:
            res = mm(GP[0], W[0], NT)
            for k in range(1, 4):
                res = res + mm(GP[k], W[k], NT)
        OUTP[o] = res
        for s in range(2):
            rows = pl.ds(pl.multiple_of(256 * s + other_rows, 128), 128)
            op.append(remote(OUTP.at[o, rows, :], RP.at[o, s], op_send.at[o, s], op_recv.at[o, s], partner))
    zh_start(0)
    xy_start(3)
    small_y()
    for o, ref in enumerate((out_ref, grad_ref)):
        for s in range(2):
            op[2 * o + s].wait_recv()
            rows = pl.ds(pl.multiple_of(256 * s + 128 * c, 128), 128)
            value = (OUTP[o, rows, :] + RP[o, s]).astype(BF16)
            ref[s] = value if s == 0 else mm(value, FLIP[...]).astype(BF16)
    zh_start(1)
    xg_start(0)
    small_h()
    zh_start(2)
    xg_start(1)
    zh_start(3)
    small_x()
    xg_start(2)
    xg_start(3)
    for copy in pair + halo + op:
        copy.wait_send()
    for m in range(4):
        gather_sent(m)
    small_last()
    for k in range(4):
        reduced(k)
    for k in range(4):
        gout_ref[pl.ds(16 * k, 16), :] = GO[k].astype(F32) * scale
    rows = []
    for cc in range(2):
        for s in range(3):
            rows.append(jnp.concatenate([FIN[k, cc, :, pl.ds(128 * s, 128)] for k in range(4)], axis=1))
    back = mm(jnp.concatenate(rows, axis=0), QM[...], NT) * scale
    for s in range(3):
        for t in range(4):
            lanes = slice(128 * t, 128 * t + 128)
            first, second = halves(back[32 * s:32 * s + 32, lanes], back[96 + 32 * s:128 + 32 * s, lanes])
            gin_ref[:, pl.ds(s * 1024 + t * 256, 128)] = first
            gin_ref[:, pl.ds(s * 1024 + t * 256 + 128, 128)] = second
    for k in range(4):
        reduce_sent(k)
    small_sent()


def hand_over(*refs):
    n = 6
    sems = refs[2 * n]
    copies = [pltpu.make_async_copy(refs[i], refs[n + i], sems.at[i]) for i in range(n)]
    for copy in copies:
        copy.start()
    for copy in copies:
        copy.wait()


def shards(strands, cotangent, proj_in, proj_out, short_taps, filters):
    length = strands.shape[1] * lax.axis_size(("seq", "ch"))
    scale = float(length) ** (-0.5)
    dma = pltpu.SemaphoreType.DMA
    outs = (
        jax.ShapeDtypeStruct((2, 128, 512), BF16),
        jax.ShapeDtypeStruct((2, 128, 512), BF16),
        jax.ShapeDtypeStruct((32, 3072), F32),
        jax.ShapeDtypeStruct((64, 512), F32),
        jax.ShapeDtypeStruct((4, 192), F32),
        jax.ShapeDtypeStruct((4, 128), F32),
    )
    scratch = [
        pltpu.VMEM((2, 128, 512), BF16),
        pltpu.VMEM((2, 128, 512), BF16),
        pltpu.VMEM((32, 3072), BF16),
        pltpu.VMEM((64, 512), BF16),
        pltpu.VMEM((4, 3072), F32),
        pltpu.VMEM((64, 128), BF16),
    ]
    scratch += [
        pltpu.VMEM((2, 544, 512), BF16),
        pltpu.VMEM((2, 400, 512), BF16),
        pltpu.VMEM((4, 512, 384), BF16),
        pltpu.VMEM((4, 8, 16, 512), BF16),
        pltpu.VMEM((4, 32, 384), BF16),
        pltpu.VMEM((512, 512), BF16),
        pltpu.VMEM((512, 512), BF16),
        pltpu.VMEM((4, 4, 384), F32),
        pltpu.VMEM((4, 1024, 256), BF16),
        pltpu.VMEM((4, 1024, 256), BF16),
        pltpu.VMEM((512, 512), BF16),
        pltpu.VMEM((4, 512, 128), BF16),
        pltpu.VMEM((4, 512, 384), BF16),
        pltpu.VMEM((4, 8, 4, 16, 512), F32),
        pltpu.VMEM((4, 4, 384), F32),
        pltpu.VMEM((4, 8, 256), F32),
        pltpu.VMEM((12, 432, 128), F32),
        pltpu.VMEM((2, 512, 512), F32),
        pltpu.VMEM((2, 2, 128, 512), F32),
        pltpu.VMEM((4, 4, 4, 16, 512), BF16),
        pltpu.VMEM((4, 4, 4, 16, 512), BF16),
        pltpu.VMEM((4, 4, 4, 16, 512), BF16),
        pltpu.VMEM((4, 15, 16, 512), BF16),
        pltpu.VMEM((4, 4, 16, 512), BF16),
        pltpu.VMEM((4, 16, 512), BF16),
        pltpu.VMEM((4, 2, 32, 384), BF16),
        pltpu.VMEM((4, 16, 512), BF16),
        pltpu.VMEM((8, 16, 128), F32),
        pltpu.VMEM((4, 16, 128), F32),
        pltpu.VMEM((4, 16, 128), F32),
        pltpu.VMEM((3, 16, 128), F32),
        pltpu.VMEM((4, 16, 128), F32),
        pltpu.VMEM((2, 4, 16, 128), F32),
    ]
    scratch += [
        dma((6,)), dma((4,)), dma((4,)), dma((6,)), dma((6,)), dma((3,)), dma((3,)),
        dma((4,)), dma((4, 3)), dma((4,)), dma((4, 3)),
        dma((4,)), dma((4, 2)), dma((4,)), dma((4,)), dma((4,)), dma((4,)), dma((4,)), dma((4,)), dma((4,)), dma((4,)),
        dma((4,)), dma((4,)), dma((2, 2)), dma((2, 2)),
    ]
    anywhere = pl.BlockSpec(memory_space=pl.ANY)
    results = pl.pallas_call(
        functools.partial(kernel, scale),
        out_shape=tuple(pltpu.VMEM(o.shape, o.dtype) for o in outs),
        in_specs=[pl.BlockSpec(memory_space=pltpu.HBM)] * 6,
        out_specs=tuple([pl.BlockSpec(memory_space=pltpu.VMEM)] * 6),
        scratch_shapes=scratch,
        compiler_params=pltpu.CompilerParams(
            collective_id=0, has_side_effects=True, vmem_limit_bytes=56 * 2**20
        ),
        cost_estimate=pl.CostEstimate(flops=9 * 10**9, bytes_accessed=4 * 10**6, transcendentals=0),
    )(strands, cotangent, proj_in, proj_out, short_taps.T, filters)
    results = pl.pallas_call(
        hand_over,
        out_shape=outs,
        in_specs=[pl.BlockSpec(memory_space=pltpu.VMEM)] * 6,
        out_specs=tuple([anywhere] * 6),
        scratch_shapes=[dma((6,))],
    )(*[pltpu.with_memory_space_constraint(r, pltpu.VMEM) for r in results])
    return results[:4] + (results[4].T, results[5])


def solution(mesh):
    placed = P(None, ("seq", "ch"), None)
    rows = P("ch", None)
    return jax.shard_map(
        shards,
        mesh=mesh,
        in_specs=(placed, placed, rows, rows, P(), P()),
        out_specs=(placed, placed, rows, rows, rows, rows),
        check_vma=False,
    )
```

```python
import functools

import jax
import jax.numpy as jnp
from jax import lax
from jax.experimental import pallas as pl
from jax.experimental.pallas import tpu as pltpu
from jax.sharding import PartitionSpec as P

F32 = jnp.float32
BF16 = jnp.bfloat16
NN = (((1,), (0,)), ((), ()))
NT = (((1,), (1,)), ((), ()))
TN = (((0,), (0,)), ((), ()))


def mm(a, b, dims=NN):
    return lax.dot_general(a, b, dims, preferred_element_type=F32)


def lane_group(shape, span):
    return (lax.broadcasted_iota(jnp.int32, shape, 1) % span) // 16


def halves(tile, other):
    lane = lax.broadcasted_iota(jnp.int32, tile.shape, 1)
    low = jnp.where(lane < 64, tile, pltpu.roll(other, 64, 1))
    high = jnp.where(lane < 64, pltpu.roll(tile, 64, 1), other)
    return low, high


def build_tables(filters, TF, TB):
    t = lax.broadcasted_iota(jnp.int32, (128, 256), 0)
    k = lax.broadcasted_iota(jnp.int32, (128, 256), 1)
    to_f = jnp.where(t + k == 128, 1.0, 0.0).astype(BF16)
    to_b = jnp.where(t == k, 1.0, 0.0).astype(BF16)
    pat_f = mm(filters, to_f)
    pat_b = mm(filters, to_b)
    for g in range(32):
        for pat, table in ((pat_f, TF), (pat_b, TB)):
            rows = jnp.broadcast_to(pat[g:g + 1], (128, 256))
            skewed = pltpu.roll(rows, 0, 1, stride=1, stride_axis=0)
            table[g // 8, pl.ds((g % 8) * 128, 128), :] = skewed.astype(BF16)


def anti_identity(n):
    r = lax.broadcasted_iota(jnp.int32, (n, n), 0)
    c = lax.broadcasted_iota(jnp.int32, (n, n), 1)
    return jnp.where(r + c == n - 1, 1.0, 0.0).astype(BF16)


def diag(products, rows, count):
    group = lane_group((rows, products.shape[1]), 16 * count)
    out = products[0:rows]
    for g in range(1, count):
        out = jnp.where(group == g, products[g * rows:(g + 1) * rows], out)
    return out


def compute_chunk(k, U, C, Win, Wout, taps_ref, TF, TB, UT, HID, GP, PART, PSH, PFIL, ROWS, hook_a, hook_b):
    w = Win[k]
    wo = Wout[k].reshape(128, 512)
    taps = taps_ref[k]
    tf = TF[k]
    tb = TB[k]
    own_proj, gated, gc, keys, values, queries, ghs = [], [], [], [], [], [], []
    for s in range(2):
        sign = 1 if s == 0 else -1
        kv_at = 0 if s == 0 else 128
        q_at = 128 - kv_at
        pkv = mm(U[s, pl.ds(kv_at, 416), :], w[:, 128:]).astype(BF16)
        pq = mm(U[s, pl.ds(q_at, 416), :], w[:, :128]).astype(BF16)
        gh = mm(C[s], wo, NT).astype(BF16).astype(F32)
        mixed = []
        own_kv = 144 if s == 0 else 16
        own_q = 160 - own_kv
        for part, values_in in enumerate((pq, pkv[:, :128], pkv[:, 128:])):
            held = ROWS.at[3 * s + part]
            wide = values_in.astype(F32)
            held[pl.ds(8, 416), :] = wide
            t = taps[:, 128 * part:128 * part + 128]
            total = t[0:1] * wide
            for j in range(1, 4):
                total = total + t[j:j + 1] * held[pl.ds(8 - sign * j, 416), :]
            mixed.append(total)
        mq, key, value = mixed
        own_proj.append((own_q, own_kv, own_kv))
        gated.append((key * value).astype(BF16))
        keys.append(key)
        values.append(value)
        queries.append(mq)
        ghs.append(gh)
        at = 16 if s == 0 else 0
        gc.append((gh * mq[at:at + 400]).astype(BF16))
    hook_a()
    def packed(first, second):
        low_first, high_first = halves(*first)
        low_second, high_second = halves(*second)
        return (
            jnp.concatenate([low_first, low_second], axis=1),
            jnp.concatenate([high_first, high_second], axis=1),
        )

    def blocks_of(value, at, rows):
        return value[at:at + rows], value[at + 128:at + 128 + rows]

    xf = packed(blocks_of(gated[0], 16, 256), blocks_of(gc[1], 16, 256))
    xb = packed(blocks_of(gc[0], 0, 256), blocks_of(gated[1], 16, 256))
    left = packed(blocks_of(gc[0], 0, 128), blocks_of(gated[1], 16, 128))
    reverse = anti_identity(128)
    group = lane_group((128, 256), 64)
    yf, yb, prods = [], [], []
    for h in range(2):
        yf.append(diag(mm(tf[512 * h:512 * h + 512], xf[h]), 128, 4))
        yb.append(diag(mm(tb[512 * h:512 * h + 512], xb[h]), 128, 4))
        turned = mm(reverse, left[h]).astype(BF16)
        masked = jnp.concatenate([jnp.where(group == g, turned, jnp.zeros_like(turned)) for g in range(4)], axis=0)
        prods.append(mm(masked, xf[h], NT))
    f_first_strand = halves(yf[0][:, :128], yf[1][:, :128])
    f_second_strand = halves(yf[0][:, 128:], yf[1][:, 128:])
    b_first_strand = halves(yb[0][:, :128], yb[1][:, :128])
    b_second_strand = halves(yb[0][:, 128:], yb[1][:, 128:])
    tf3 = tf.reshape(8, 128, 256)
    tb3 = tb.reshape(8, 128, 256)
    f_last = tf3[:, 112:].reshape(128, 256)
    f_first = tf3[:, :16].reshape(128, 256)
    b_last = tb3[:, 112:].reshape(128, 256)
    b_first = tb3[:, :16].reshape(128, 256)
    conv0_x = diag(mm(f_last, gated[0][160:416]), 16, 8)
    gg1_x = diag(mm(f_first, gc[1][0:256]), 16, 8)
    gg0_x = diag(mm(b_last, gc[0][144:400]), 16, 8)
    conv1_x = diag(mm(b_first, gated[1][0:256]), 16, 8)
    conv = [
        jnp.concatenate([*f_first_strand, conv0_x], axis=0),
        jnp.concatenate([conv1_x, *b_second_strand], axis=0),
    ]
    gg = [
        jnp.concatenate([*b_first_strand, gg0_x], axis=0),
        jnp.concatenate([gg1_x, *f_second_strand], axis=0),
    ]
    hook_b()
    short = [[None] * 3 for _ in range(4)]
    for s in range(2):
        sign = 1 if s == 0 else -1
        own = 0 if s == 0 else 16
        q_at = 16 if s == 0 else 128
        kv_at = 144 if s == 0 else 0
        gh_at = 0 if s == 0 else 128
        query = queries[s][q_at:q_at + 272]
        hidden = (query[own:own + 256] * conv[s][own:own + 256]).astype(BF16)
        HID[k, pl.ds(256 * s, 256), :] = hidden
        grads = (
            ghs[s][gh_at:gh_at + 272] * conv[s],
            gg[s] * values[s][kv_at:kv_at + 272],
            gg[s] * keys[s][kv_at:kv_at + 272],
        )
        for part in range(3):
            held = ROWS.at[6 + 3 * s + part]
            p_own = ROWS[3 * s + part, pl.ds(8 + own_proj[s][part], 256), :]
            gm = grads[part].astype(BF16).astype(F32)
            held[pl.ds(8, 272), :] = gm
            t = taps[:, 128 * part:128 * part + 128]
            total = None
            for j in range(4):
                moved = gm[own:own + 256] if j == 0 else held[pl.ds(8 + own + sign * j, 256), :]
                term = t[j:j + 1] * moved
                total = term if total is None else total + term
                column = jnp.sum(p_own * moved, axis=0, keepdims=True)
                short[j][part] = column if s == 0 else short[j][part] + column
            GP[k, pl.ds(256 * s, 256), pl.ds(128 * part, 128)] = total.astype(BF16)
    for j in range(4):
        for part in range(3):
            PSH[k, pl.ds(j, 1), pl.ds(128 * part, 128)] = short[j][part]
    PART[k, :, :, :, pl.ds(0, 384)] = mm(UT[...], GP[k]).reshape(8, 4, 16, 384)
    po = mm(HID[k, pl.ds(0, 256), :], C[0, pl.ds(0, 256), :], TN)
    po = po + mm(HID[k, pl.ds(256, 256), :], C[1, pl.ds(144, 256), :], TN)
    for q in range(4):
        PART[k, :, q, :, pl.ds(384, 128)] = po[:, 128 * q:128 * q + 128].reshape(8, 16, 128)
    rows = []
    for g in range(8):
        r = pltpu.roll(prods[g // 4][128 * (g % 4):128 * (g % 4) + 128], 129, 1, stride=1, stride_axis=0)
        rows.append(jnp.sum(r, axis=0, keepdims=True))
    PFIL[k] = jnp.concatenate(rows, axis=0)


MESH = pl.DeviceIdType.MESH


def remote(src, dst, send, recv, device):
    copy = pltpu.make_async_remote_copy(
        src_ref=src, dst_ref=dst, send_sem=send, recv_sem=recv, device_id=device, device_id_type=MESH
    )
    copy.start()
    return copy


def wait_bytes(ref, sem):
    pltpu.make_async_copy(ref, ref, sem).wait()


def at_coords(x, y, z, c):
    return ((z // 2) * 4 + x, (z % 2) * 8 + y * 2 + c)


def at_chip(p, c):
    return (p // 8, (p % 8) * 2 + c)


def split_cores(wide):
    low, high = [], []
    for t in range(4):
        a, b = halves(wide[:, 256 * t:256 * t + 128], wide[:, 256 * t + 128:256 * t + 256])
        low.append(a)
        high.append(b)
    return jnp.concatenate(low, axis=1), jnp.concatenate(high, axis=1)


def exact_dot(value, zero_one, dims=NN):
    first = value.astype(BF16)
    rest = value - first.astype(F32)
    second = rest.astype(BF16)
    third = (rest - second.astype(F32)).astype(BF16)
    return mm(first, zero_one, dims) + mm(second, zero_one, dims) + mm(third, zero_one, dims)


def block_order():
    row = lax.broadcasted_iota(jnp.int32, (512, 512), 0)
    col = lax.broadcasted_iota(jnp.int32, (512, 512), 1)
    goes = ((row // 16) % 4) * 128 + (row // 64) * 16 + row % 16
    return jnp.where(goes == col, 1.0, 0.0).astype(BF16)


def kernel(
    scale,
    strands_hbm, cotangent_hbm, proj_in_hbm, proj_out_hbm, taps_hbm, filters_hbm,
    out_ref, grad_ref, gin_ref, gout_ref, gshort_ref, gfil_ref,
    strands, cotangent, proj_in, proj_out, taps_in, filters_in,
    U, C, W, WO, WSEND, QM, FLIP, TAPS, TF, TB, UT, HID, GP, PART, PSH, PFIL, ROWS, OUTP, RP,
    SZ, RZ, SXY, RXY, ZH, FS, FIN, GO,
    SMP, SMZ, SMY, SMYR, SMH, SMX,
    in_sem, pair_send, pair_recv, halo_send, halo_recv, fwd_send, fwd_recv,
    w_send, w_recv, wo_send, wo_recv,
    z_send, z_recv, xy_send, xy_recv, zh_send, zh_recv, xg_send, xg_recv, go_send, go_recv,
    sm_send, sm_recv, op_send, op_recv,
):
    arrivals = []
    for i, (src, dst) in enumerate((
        (proj_in_hbm, proj_in), (proj_out_hbm, proj_out), (strands_hbm, strands),
        (cotangent_hbm, cotangent), (taps_hbm, taps_in), (filters_hbm, filters_in),
    )):
        copy = pltpu.make_async_copy(src, dst, in_sem.at[i])
        copy.start()
        arrivals.append(copy)
    seq, ch = lax.axis_index("seq"), lax.axis_index("ch")
    z_hi, x = seq // 4, seq % 4
    z_lo, y, c = ch // 8, (ch // 2) % 4, ch % 2
    z = z_hi * 2 + z_lo
    b = z_lo * 4 + y
    chip = seq * 8 + b
    before, after = (chip + 127) % 128, (chip + 1) % 128
    partner = at_coords(x, y, z, 1 - c)
    z_above, z_below = (z + 1) % 8, (z + 7) % 8
    z_up, z_down = at_coords(x, y, z_above, c), at_coords(x, y, z_below, c)
    is_first = c == 0

    barrier = pltpu.get_barrier_semaphore()
    peers = [partner]
    for zz in (z_above, z_below):
        for cc in (0, 1):
            peers.append(at_coords(x, y, zz, cc))
    for dx in range(4):
        for dy in range(4):
            if dx or dy:
                peers.append(at_coords((x + dx) % 4, (y + dy) % 4, z, c))
    for d in range(1, 4):
        peers.append(at_coords(x, y, (z + 2 * d) % 8, c))
        peers.append(at_coords((x + d) % 4, y, z, 1 - c))
        peers.append(at_coords(x, (y + d) % 4, z, 1 - c))
    for q in (before, after):
        peers.append(at_chip(q, 0))
        peers.append(at_chip(q, 1))
    for peer in peers:
        pl.semaphore_signal(barrier, inc=1, device_id=peer, device_id_type=MESH)

    QM[...] = block_order()
    FLIP[...] = anti_identity(512)
    my_rows = pl.multiple_of(64 * b + 32 * c, 32)
    arrivals[0].wait()
    low, high = [], []
    for s in range(3):
        a, o = split_cores(proj_in[:, pl.ds(s * 1024, 1024)].astype(F32))
        low.append(a)
        high.append(o)
    moved = mm(jnp.concatenate(low + high, axis=0).astype(BF16), QM[...])
    for k in range(4):
        for s in range(3):
            lanes = pl.ds(128 * s, 128)
            even = moved[32 * s:32 * s + 32, 128 * k:128 * k + 128]
            odd = moved[96 + 32 * s:128 + 32 * s, 128 * k:128 * k + 128]
            W[k, pl.ds(my_rows, 32), lanes] = jnp.where(is_first, even, odd).astype(BF16)
            WSEND[k, :, lanes] = jnp.where(is_first, odd, even).astype(BF16)
    arrivals[1].wait()
    for k in range(4):
        WO[k, b] = proj_out[pl.ds(16 * k, 16), :]
    own = pl.multiple_of(144 + 128 * c, 16)
    own_c0 = pl.multiple_of(128 * c, 16)
    arrivals[2].wait()
    U[0, pl.ds(own, 128), :] = strands[0]
    U[1, pl.ds(own, 128), :] = mm(strands[1], FLIP[...]).astype(BF16)
    arrivals[3].wait()
    C[0, pl.ds(own_c0, 128), :] = cotangent[0]
    C[1, pl.ds(own, 128), :] = mm(cotangent[1], FLIP[...]).astype(BF16)
    arrivals[4].wait()
    arrivals[5].wait()
    pl.semaphore_wait(barrier, len(peers))

    def wo_half(m, bb, half):
        return WO.at[m, bb, :, pl.ds(256 * half, 256)]

    def w_half(m, bb, half):
        return W.at[m, pl.ds(pl.multiple_of(64 * bb + 32 * half, 32), 32), :]

    def gather_first(m):
        mine = W.at[m, pl.ds(my_rows, 32), :]
        theirs = WSEND.at[m]
        place = W.at[m, pl.ds(my_rows, 32), :]
        remote(theirs, place, w_send.at[m], w_recv.at[m, 0], partner)
        for d in (1, 3, 2):
            yy = (y + d) % 4
            kind = 2 if d == 2 else 0
            remote(mine, place, w_send.at[m], w_recv.at[m, kind], at_coords(x, yy, z, c))
            remote(theirs, place, w_send.at[m], w_recv.at[m, kind], at_coords(x, yy, z, 1 - c))
            remote(WO.at[m, b], WO.at[m, b], wo_send.at[m], wo_recv.at[m, kind], at_coords(x, yy, z, c))
        z_side = jnp.where(is_first, z_above, z_below)
        remote(mine, place, w_send.at[m], w_recv.at[m, 1], at_coords(x, y, z_side, c))
        remote(theirs, place, w_send.at[m], w_recv.at[m, 1], at_coords(x, y, z_side, 1 - c))
        for half, side in ((0, z_up), (1, z_down)):
            remote(wo_half(m, b, half), wo_half(m, b, half), wo_send.at[m], wo_recv.at[m, 1], side)

    def gather_second(m):
        wait_bytes(W.at[m, pl.ds(0, 160), :], w_recv.at[m, 0])
        wait_bytes(WO.at[m, pl.ds(0, 2)], wo_recv.at[m, 0])
        for d in (1, 3, 2):
            if d == 2:
                wait_bytes(W.at[m, pl.ds(0, 64), :], w_recv.at[m, 2])
                wait_bytes(WO.at[m, 0], wo_recv.at[m, 2])
            bb = z_lo * 4 + (y + d) % 4
            for half, side in ((0, z_up), (1, z_down)):
                remote(w_half(m, bb, half), w_half(m, bb, half), w_send.at[m], w_recv.at[m, 1], side)
                remote(wo_half(m, bb, half), wo_half(m, bb, half), wo_send.at[m], wo_recv.at[m, 1], side)

    def gather_last(m):
        wait_bytes(W.at[m, pl.ds(0, 256), :], w_recv.at[m, 1])
        wait_bytes(WO.at[m, pl.ds(0, 4)], wo_recv.at[m, 1])

    def gather_sent(m):
        wait_bytes(W.at[m, pl.ds(0, 480), :], w_send.at[m])
        wait_bytes(WO.at[m, pl.ds(0, 7)], wo_send.at[m])

    gather_first(0)

    far = jnp.where(is_first, before, after)
    near = jnp.where(is_first, after, before)
    big_at = pl.multiple_of(jnp.where(is_first, 400, 16), 16)
    small_src = pl.multiple_of(own + jnp.where(is_first, 112, 0), 16)
    small_at = pl.multiple_of(jnp.where(is_first, 0, 528), 16)
    halo = []
    for s in range(2):
        halo.append(remote(
            U.at[s, pl.ds(own, 128), :], U.at[s, pl.ds(big_at, 128), :],
            halo_send.at[s], halo_recv.at[1 - c], at_chip(far, s)))
        halo.append(remote(
            U.at[s, pl.ds(small_src, 16), :], U.at[s, pl.ds(small_at, 16), :],
            halo_send.at[2 + s], halo_recv.at[2 + c], at_chip(near, s)))
    c_own = pl.multiple_of(jnp.where(is_first, 0, 272), 16)
    c_big = pl.multiple_of(jnp.where(is_first, 256, 16), 16)
    halo.append(remote(
        C.at[c, pl.ds(c_own, 128), :], C.at[c, pl.ds(c_big, 128), :],
        halo_send.at[4], halo_recv.at[4], at_chip(far, c)))
    c_small_src = pl.multiple_of(jnp.where(is_first, 144 + 112, 128), 16)
    c_small = pl.multiple_of(jnp.where(is_first, 0, 384), 16)
    halo.append(remote(
        C.at[1 - c, pl.ds(c_small_src, 16), :], C.at[1 - c, pl.ds(c_small, 16), :],
        halo_send.at[5], halo_recv.at[5], at_chip(near, 1 - c)))
    pair = [
        remote(U.at[s, pl.ds(own, 128), :], U.at[s, pl.ds(own, 128), :], pair_send.at[s], pair_recv.at[s], partner)
        for s in range(2)
    ]
    pair.append(remote(
        C.at[0, pl.ds(own_c0, 128), :], C.at[0, pl.ds(own_c0, 128), :], pair_send.at[2], pair_recv.at[2], partner))
    pair.append(remote(
        C.at[1, pl.ds(own, 128), :], C.at[1, pl.ds(own, 128), :], pair_send.at[3], pair_recv.at[3], partner))
    for m in range(1, 4):
        gather_first(m)

    picked = []
    for s in range(3):
        a, o = split_cores(taps_in[:, pl.ds(s * 1024, 1024)])
        picked.append(jnp.where(is_first, a, o))
    picked = exact_dot(jnp.concatenate(picked, axis=0), QM[...])
    for k in range(4):
        for s in range(3):
            TAPS[k, :, pl.ds(128 * s, 128)] = picked[4 * s:4 * s + 4, 128 * k:128 * k + 128]
    row = lax.broadcasted_iota(jnp.int32, (32, 64), 0)
    col = lax.broadcasted_iota(jnp.int32, (32, 64), 1)
    chosen = jnp.where((row % 8) * 8 + 4 * c + row // 8 == col, 1.0, 0.0).astype(BF16)
    build_tables(mm(chosen, filters_in[...]).astype(BF16), TF, TB)

    gather_second(0)
    wait_bytes(U.at[c, pl.ds(16, 128), :], halo_recv.at[0])
    wait_bytes(U.at[c, pl.ds(400, 128), :], halo_recv.at[1])
    wait_bytes(U.at[c, pl.ds(0, 16), :], halo_recv.at[2])
    wait_bytes(U.at[c, pl.ds(528, 16), :], halo_recv.at[3])
    wait_bytes(C.at[c, pl.ds(c_big, 128), :], halo_recv.at[4])
    wait_bytes(C.at[c, pl.ds(pl.multiple_of(jnp.where(is_first, 384, 0), 16), 16), :], halo_recv.at[5])
    c_halo = pl.multiple_of(jnp.where(is_first, 256, 0), 16)
    c_halo_other = pl.multiple_of(jnp.where(is_first, 0, 256), 16)
    fwd = []
    for i, at in enumerate((0, 400)):
        rows = U.at[c, pl.ds(at, 144), :]
        fwd.append(remote(rows, rows, fwd_send.at[i], fwd_recv.at[i], partner))
    rows = C.at[c, pl.ds(c_halo, 144), :]
    fwd.append(remote(rows, rows, fwd_send.at[2], fwd_recv.at[2], partner))
    for copy in pair:
        copy.wait_recv()
    for s in range(2):
        UT[:, pl.ds(256 * s, 256)] = jnp.transpose(U[s, pl.ds(144, 256), :])
    gather_second(1)
    for i, at in enumerate((0, 400)):
        wait_bytes(U.at[1 - c, pl.ds(at, 144), :], fwd_recv.at[i])
    wait_bytes(C.at[1 - c, pl.ds(c_halo_other, 144), :], fwd_recv.at[2])
    for copy in fwd:
        copy.wait_send()

    @pl.when(chip == 0)
    def _():
        U[:, pl.ds(0, 144), :] = jnp.zeros((2, 144, 512), BF16)
        C[1, pl.ds(0, 144), :] = jnp.zeros((144, 512), BF16)

    @pl.when(chip == 127)
    def _():
        U[:, pl.ds(400, 144), :] = jnp.zeros((2, 144, 512), BF16)
        C[0, pl.ds(256, 144), :] = jnp.zeros((144, 512), BF16)

    def z_start(k):
        SZ[k] = PART[k, pl.ds((1 - z_lo) * 4, 4)].astype(BF16)
        remote(SZ.at[k, :, pl.ds(0, 2)], RZ.at[k, :, pl.ds(0, 2)], z_send.at[k], z_recv.at[k, 0], z_up)
        remote(SZ.at[k, :, pl.ds(2, 2)], RZ.at[k, :, pl.ds(2, 2)], z_send.at[k], z_recv.at[k, 1], z_down)

    def xy_start(k):
        wait_bytes(RZ.at[k, :, pl.ds(0, 2)], z_recv.at[k, 0])
        wait_bytes(RZ.at[k, :, pl.ds(2, 2)], z_recv.at[k, 1])
        SXY[k] = (PART[k, pl.ds(z_lo * 4, 4)] + RZ[k].astype(F32)).astype(BF16)
        for dx in range(4):
            for dy in range(4):
                if dx or dy:
                    xx, yy = (x + dx) % 4, (y + dy) % 4
                    remote(SXY.at[k, yy, xx], RXY.at[k, 4 * dx + dy - 1],
                           xy_send.at[k], xy_recv.at[k], at_coords(xx, yy, z, c))

    def zh_start(k):
        wait_bytes(RXY.at[k], xy_recv.at[k])
        total = SXY[k, y, x].astype(F32)
        for i in range(15):
            total = total + RXY[k, i].astype(F32)
        ZH[k, z_hi] = total.astype(BF16)
        for d in range(1, 4):
            remote(ZH.at[k, z_hi], ZH.at[k, z_hi], zh_send.at[k], zh_recv.at[k], at_coords(x, y, (z + 2 * d) % 8, c))

    target = x // 2
    row_at = pl.multiple_of(16 * (x % 2), 16)
    go_at = pl.multiple_of(128 * x, 128)

    def xg_start(k):
        wait_bytes(ZH.at[k, pl.ds(0, 3)], zh_recv.at[k])
        total = ZH[k, 0].astype(F32)
        for i in range(1, 4):
            total = total + ZH[k, i].astype(F32)
        FS[k] = total.astype(BF16)
        part = FS.at[k, :, pl.ds(0, 384)]
        place = FIN.at[k, c, pl.ds(row_at, 16), :]
        piece = FS.at[k, :, pl.ds(384, 128)]
        spot = GO.at[k, :, pl.ds(go_at, 128)]
        for d in range(1, 4):
            remote(part, place, xg_send.at[k], xg_recv.at[k], at_coords((x + d) % 4, y, z, target))
            remote(piece, spot, go_send.at[k], go_recv.at[k], at_coords((x + d) % 4, y, z, c))

        @pl.when(c == target)
        def _():
            pltpu.make_async_copy(part, place, xg_recv.at[k]).start()

        @pl.when(c != target)
        def _():
            remote(part, place, xg_send.at[k], xg_recv.at[k], partner)

        GO[k, :, pl.ds(go_at, 128)] = FS[k, :, pl.ds(384, 128)]

    def reduced(k):
        wait_bytes(FIN.at[k], xg_recv.at[k])
        wait_bytes(GO.at[k, :, pl.ds(0, 384)], go_recv.at[k])

    def reduce_sent(k):
        wait_bytes(SZ.at[k], z_send.at[k])
        wait_bytes(RXY.at[k], xy_send.at[k])
        wait_bytes(ZH.at[k, pl.ds(0, 3)], zh_send.at[k])
        wait_bytes(FS.at[pl.ds(0, 3), :, pl.ds(0, 384)], xg_send.at[k])
        wait_bytes(FS.at[pl.ds(0, 3), :, pl.ds(384, 128)], go_send.at[k])

        @pl.when(c != target)
        def _():
            wait_bytes(FS.at[k, :, pl.ds(0, 384)], xg_send.at[k])

    def small_z():
        taps_rows = []
        for k in range(4):
            taps_rows.append(jnp.concatenate(
                [PSH[k, :, pl.ds(128 * s, 128)] for s in range(3)], axis=0))
        back = exact_dot(jnp.concatenate(taps_rows, axis=1), QM[...], NT)
        fil = [pltpu.roll(PFIL[k], 255, 1)[:, :128] for k in range(4)]
        for i in range(8):
            m = i // 2
            tiles = (3 * m, 3 * m + 1) if i % 2 == 0 else (3 * m + 1, 3 * m + 2)
            rows = []
            for t in tiles:
                s, p = t // 4, t % 4
                rows.append(back[4 * s:4 * s + 4, 128 * p:128 * p + 128])
            rows += [fil[k][i:i + 1] for k in range(4)]
            SMP[i] = jnp.concatenate(rows + [jnp.zeros((4, 128), F32)], axis=0)
        remote(SMP.at[pl.ds((1 - z_lo) * 4, 4)], SMZ, sm_send.at[0], sm_recv.at[0], z_up)

    def small_y():
        wait_bytes(SMZ, sm_recv.at[0])
        SMY[...] = SMP[pl.ds(z_lo * 4, 4)] + SMZ[...]
        for d in range(1, 4):
            yy = (y + d) % 4
            remote(SMY.at[yy], SMYR.at[d - 1], sm_send.at[1], sm_recv.at[1], at_coords(x, yy, z, c))

    def small_h():
        wait_bytes(SMYR, sm_recv.at[1])
        SMH[z_hi] = SMY[y] + SMYR[0] + SMYR[1] + SMYR[2]
        for d in range(1, 4):
            remote(SMH.at[z_hi], SMH.at[z_hi], sm_send.at[2], sm_recv.at[2], at_coords(x, y, (z + 2 * d) % 8, c))

    def small_x():
        wait_bytes(SMH.at[pl.ds(0, 3)], sm_recv.at[2])
        SMX[c, x] = SMH[0] + SMH[1] + SMH[2] + SMH[3]
        for d in range(1, 4):
            for cc in (c, 1 - c):
                remote(SMX.at[c, x], SMX.at[c, x], sm_send.at[3], sm_recv.at[3], at_coords((x + d) % 4, y, z, cc))
        remote(SMX.at[c, x], SMX.at[c, x], sm_send.at[3], sm_recv.at[3], partner)

    def small_last():
        wait_bytes(SMP.at[pl.ds(0, 7)], sm_recv.at[3])
        e = SMX[0, 0] + SMX[0, 1] + SMX[0, 2] + SMX[0, 3]
        o = SMX[1, 0] + SMX[1, 1] + SMX[1, 2] + SMX[1, 3]
        mine = jnp.where(is_first, e, o)
        gfil_ref[...] = exact_dot(mine, anti_identity(128))[8:12] * scale
        lane = lax.broadcasted_iota(jnp.int32, (4, 128), 1)

        def blocks(v):
            a, t = v[0:4], v[4:8]
            turned_a, turned_t = pltpu.roll(a, 64, 1), pltpu.roll(t, 64, 1)
            even = b % 2 == 0
            return (
                jnp.where(even, a, turned_a),
                jnp.where(even, turned_a, t),
                jnp.where(even, t, turned_t),
            )

        e, o = blocks(e), blocks(o)
        one = jnp.where(is_first, e[0], o[1])
        two = jnp.where(is_first, o[0], e[2])
        three = jnp.where(is_first, e[1], o[2])
        gshort_ref[:, pl.ds(0, 128)] = jnp.where(lane < 64, one, pltpu.roll(two, 64, 1)) * scale
        gshort_ref[:, pl.ds(128, 64)] = three[:, :64] * scale

    def small_sent():
        wait_bytes(SMZ, sm_send.at[0])
        wait_bytes(SMYR, sm_send.at[1])
        wait_bytes(SMYR, sm_send.at[2])
        wait_bytes(SMP.at[pl.ds(0, 7)], sm_send.at[3])


    def body(k, carry):
        gather_last(k)

        def hook_a():
            @pl.when(k == 0)
            def _():
                gather_second(2)

            @pl.when(k == 1)
            def _():
                gather_second(3)

        def hook_b():
            pass

        compute_chunk(k, U, C, W, WO, TAPS, TF, TB, UT, HID, GP, PART, PSH, PFIL, ROWS, hook_a, hook_b)
        z_start(k)

        @pl.when(k >= 2)
        def _():
            xy_start(k - 2)

        return carry

    lax.fori_loop(0, 4, body, 0)

    small_z()
    other_rows = 128 * (1 - c)
    op = []
    for o in range(2):
        if o == 0:
            res = mm(HID[0], WO[0].reshape(128, 512))
            for k in range(1, 4):
                res = res + mm(HID[k], WO[k].reshape(128, 512))
            xy_start(2)
        else:
            res = mm(GP[0], W[0], NT)
            for k in range(1, 4):
                res = res + mm(GP[k], W[k], NT)
        OUTP[o] = res
        for s in range(2):
            rows = pl.ds(pl.multiple_of(256 * s + other_rows, 128), 128)
            op.append(remote(OUTP.at[o, rows, :], RP.at[o, s], op_send.at[o, s], op_recv.at[o, s], partner))
    zh_start(0)
    xy_start(3)
    small_y()
    for o, ref in enumerate((out_ref, grad_ref)):
        for s in range(2):
            op[2 * o + s].wait_recv()
            rows = pl.ds(pl.multiple_of(256 * s + 128 * c, 128), 128)
            value = (OUTP[o, rows, :] + RP[o, s]).astype(BF16)
            ref[s] = value if s == 0 else mm(value, FLIP[...]).astype(BF16)
    zh_start(1)
    xg_start(0)
    small_h()
    zh_start(2)
    xg_start(1)
    zh_start(3)
    small_x()
    xg_start(2)
    xg_start(3)
    for copy in pair + halo + op:
        copy.wait_send()
    for m in range(4):
        gather_sent(m)
    small_last()
    def projected_back(k):
        rows = [FIN[k, cc, :, pl.ds(128 * s, 128)] for cc in range(2) for s in range(3)]
        return mm(jnp.concatenate(rows, axis=0), QM[:, pl.ds(128 * k, 128)], NT)

    back = None
    for k in range(4):
        reduced(k)
        gout_ref[pl.ds(16 * k, 16), :] = GO[k].astype(F32) * scale
        term = projected_back(k)
        back = term if back is None else back + term
    for s in range(3):
        for t in range(4):
            lanes = slice(128 * t, 128 * t + 128)
            first, second = halves(back[32 * s:32 * s + 32, lanes], back[96 + 32 * s:128 + 32 * s, lanes])
            gin_ref[:, pl.ds(s * 1024 + t * 256, 128)] = first * scale
            gin_ref[:, pl.ds(s * 1024 + t * 256 + 128, 128)] = second * scale
    for k in range(4):
        reduce_sent(k)
    small_sent()


def hand_over(*refs):
    n = 6
    sems = refs[2 * n]
    copies = [pltpu.make_async_copy(refs[i], refs[n + i], sems.at[i]) for i in range(n)]
    for copy in copies:
        copy.start()
    for copy in copies:
        copy.wait()


def shards(strands, cotangent, proj_in, proj_out, short_taps, filters):
    length = strands.shape[1] * lax.axis_size(("seq", "ch"))
    scale = float(length) ** (-0.5)
    dma = pltpu.SemaphoreType.DMA
    outs = (
        jax.ShapeDtypeStruct((2, 128, 512), BF16),
        jax.ShapeDtypeStruct((2, 128, 512), BF16),
        jax.ShapeDtypeStruct((32, 3072), F32),
        jax.ShapeDtypeStruct((64, 512), F32),
        jax.ShapeDtypeStruct((4, 192), F32),
        jax.ShapeDtypeStruct((4, 128), F32),
    )
    scratch = [
        pltpu.VMEM((2, 128, 512), BF16),
        pltpu.VMEM((2, 128, 512), BF16),
        pltpu.VMEM((32, 3072), BF16),
        pltpu.VMEM((64, 512), BF16),
        pltpu.VMEM((4, 3072), F32),
        pltpu.VMEM((64, 128), BF16),
    ]
    scratch += [
        pltpu.VMEM((2, 544, 512), BF16),
        pltpu.VMEM((2, 400, 512), BF16),
        pltpu.VMEM((4, 512, 384), BF16),
        pltpu.VMEM((4, 8, 16, 512), BF16),
        pltpu.VMEM((4, 32, 384), BF16),
        pltpu.VMEM((512, 512), BF16),
        pltpu.VMEM((512, 512), BF16),
        pltpu.VMEM((4, 4, 384), F32),
        pltpu.VMEM((4, 1024, 256), BF16),
        pltpu.VMEM((4, 1024, 256), BF16),
        pltpu.VMEM((512, 512), BF16),
        pltpu.VMEM((4, 512, 128), BF16),
        pltpu.VMEM((4, 512, 384), BF16),
        pltpu.VMEM((4, 8, 4, 16, 512), F32),
        pltpu.VMEM((4, 4, 384), F32),
        pltpu.VMEM((4, 8, 256), F32),
        pltpu.VMEM((12, 432, 128), F32),
        pltpu.VMEM((2, 512, 512), F32),
        pltpu.VMEM((2, 2, 128, 512), F32),
        pltpu.VMEM((4, 4, 4, 16, 512), BF16),
        pltpu.VMEM((4, 4, 4, 16, 512), BF16),
        pltpu.VMEM((4, 4, 4, 16, 512), BF16),
        pltpu.VMEM((4, 15, 16, 512), BF16),
        pltpu.VMEM((4, 4, 16, 512), BF16),
        pltpu.VMEM((4, 16, 512), BF16),
        pltpu.VMEM((4, 2, 32, 384), BF16),
        pltpu.VMEM((4, 16, 512), BF16),
        pltpu.VMEM((8, 16, 128), F32),
        pltpu.VMEM((4, 16, 128), F32),
        pltpu.VMEM((4, 16, 128), F32),
        pltpu.VMEM((3, 16, 128), F32),
        pltpu.VMEM((4, 16, 128), F32),
        pltpu.VMEM((2, 4, 16, 128), F32),
    ]
    scratch += [
        dma((6,)), dma((4,)), dma((4,)), dma((6,)), dma((6,)), dma((3,)), dma((3,)),
        dma((4,)), dma((4, 3)), dma((4,)), dma((4, 3)),
        dma((4,)), dma((4, 2)), dma((4,)), dma((4,)), dma((4,)), dma((4,)), dma((4,)), dma((4,)), dma((4,)), dma((4,)),
        dma((4,)), dma((4,)), dma((2, 2)), dma((2, 2)),
    ]
    anywhere = pl.BlockSpec(memory_space=pl.ANY)
    results = pl.pallas_call(
        functools.partial(kernel, scale),
        out_shape=tuple(pltpu.VMEM(o.shape, o.dtype) for o in outs),
        in_specs=[pl.BlockSpec(memory_space=pltpu.HBM)] * 6,
        out_specs=tuple([pl.BlockSpec(memory_space=pltpu.VMEM)] * 6),
        scratch_shapes=scratch,
        compiler_params=pltpu.CompilerParams(
            collective_id=0, has_side_effects=True, vmem_limit_bytes=56 * 2**20
        ),
        cost_estimate=pl.CostEstimate(flops=9 * 10**9, bytes_accessed=4 * 10**6, transcendentals=0),
    )(strands, cotangent, proj_in, proj_out, short_taps.T, filters)
    results = pl.pallas_call(
        hand_over,
        out_shape=outs,
        in_specs=[pl.BlockSpec(memory_space=pltpu.VMEM)] * 6,
        out_specs=tuple([anywhere] * 6),
        scratch_shapes=[dma((6,))],
    )(*[pltpu.with_memory_space_constraint(r, pltpu.VMEM) for r in results])
    return results[:4] + (results[4].T, results[5])


def solution(mesh):
    placed = P(None, ("seq", "ch"), None)
    rows = P("ch", None)
    return jax.shard_map(
        shards,
        mesh=mesh,
        in_specs=(placed, placed, rows, rows, P(), P()),
        out_specs=(placed, placed, rows, rows, rows, rows),
        check_vma=False,
    )
```
